128 devices in a mesh: dp: 8 (over x_lo, z), blk: 16 (over y, x_hi, core).
Axes of the slice: x: 4 (x_hi: 2, x_lo: 2; x = x_hi * 2 + x_lo), y: 4, z: 4, core: 2. Of those that a mesh axis runs over, the one named last changes fastest.
Arguments:
- query_matrix: bfloat16 [8, 3072, 4096], P('dp', 'blk'), may hold values from -6 to 6
- key_matrix: bfloat16 [8, 3072, 512], P('dp', 'blk'), may hold values from -6 to 6
- value_matrix: bfloat16 [8, 3072, 512], P('dp', 'blk'), may hold values from -6 to 6
- output_gradient: bfloat16 [8, 3072, 4096], P('dp', 'blk'), may hold values from -6 to 6
- log_softmax_norm: float32 [8, 32, 3072], P('dp', None, 'blk'), may hold values from 6 to 9
- output_dot_rows: float32 [8, 32, 3072], P('dp', None, 'blk'), may hold values from -48 to 48
- shared_prefix_keys: bfloat16 [256, 512], replicated, may hold values from -6 to 6
- shared_prefix_values: bfloat16 [256, 512], replicated, may hold values from -6 to 6
- prefix_len: int32 [8], P('dp'), may hold values from 64 to 256, as said below
- segments: int32 [8, 3072], P('dp'), may hold values from 0 to 7, never falling along the last dimension, each value on 1 to 768 neighbouring positions
- span_order: int32 [8, 32], P('dp'), may hold values from 0 to 31, each once within a row
Outputs:
- grad_query: bfloat16 [8, 3072, 4096], P('dp', 'blk')
- key_gradients: bfloat16 [8, 3072, 512], P('dp', 'blk')
- value_gradients: bfloat16 [8, 3072, 512], P('dp', 'blk')
- grad_prefix_key: float32 [256, 512], replicated
- grad_prefix_value: float32 [256, 512], replicated
The draws below stay inside these ranges and needn't reach their ends.
Inputs may be any that keep to these rules, and one draw needn't show every extreme that they name: `prefix_len`: each pack's prefix length; at least one pack sees all 256 prefix positions. `span_order`: each pack's row is a permutation.
All inputs are finite; a program needn't handle non-finite values.
Results may differ from the reference program's by a relative error of at most 0.0049.
Values may be sent and summed in bfloat16 or wider, within the bound.
A program may use at most 128 MiB of HBM per device.

```python
import math
import jax
import jax.numpy as jnp
import numpy as np
from jax import lax

QUERY_HEADS = 32
KEY_VALUE_HEADS = 4
HEAD_WIDTH = 128
S_DEV = 192
PREFIX_LENGTH = 256
PACK_COUNT = 8
PACK_TOKENS = 3072
SPANS = 32


def draw_prefix_len(key, part):
    key = jax.random.fold_in(key, 11)
    first, second = jax.random.split(key)
    lengths = jax.random.randint(first, (PACK_COUNT,), PREFIX_LENGTH // 4, PREFIX_LENGTH + 1)
    chosen = jax.random.randint(second, (), 0, PACK_COUNT)
    return jnp.where(jnp.arange(PACK_COUNT) == chosen, PREFIX_LENGTH, lengths).astype(jnp.int32)


def block_scale(key, shape, cuts, low, high):
    factor_of = 1.0
    for axis_at, shards_of in cuts:
        draws = jax.random.uniform(jax.random.fold_in(jax.random.fold_in(key, 6), axis_at), (shards_of,), jnp.float32, low / len(cuts), high / len(cuts))
        factor_of = factor_of * jnp.repeat(jnp.exp(draws), shape[axis_at] // shards_of).reshape((-1,) + (1,) * (len(shape) - 1 - axis_at))
    return factor_of


def profile(amount, total, reach, skew):
    weights = [(1 << 20) // math.isqrt(standing ** skew) + 1 for standing in range(2, amount + 1)]
    surplus, given = total - reach - (amount - 1), [1] * (amount - 1)
    while surplus > 0:
        candidates = [i for i in range(amount - 1) if given[i] < reach]
        pool, remaining = sum([weights[i] for i in candidates]), surplus
        for i in candidates:
            addition = min(reach - given[i], max(1, remaining * weights[i] // pool), surplus)
            given[i] = given[i] + addition
            surplus = surplus - addition
    return np.array([reach] + given)


def ragged_sizes(own_key, number_of, total, bound, skew):
    if number_of == 2:
        one = jax.random.randint(own_key, (), max(1, total - bound), min(bound, total - 1) + 1)
        return jnp.stack([one, total - one])
    tallies = jnp.asarray(profile(number_of, total, bound, skew), jnp.int32)
    twos = (number_of - 1) // 2
    donor, sink = tallies[1:1 + 2 * twos:2], tallies[2:2 + 2 * twos:2]
    margin = jnp.minimum(donor - 1, bound - sink)
    shifted = jax.random.randint(jax.random.fold_in(own_key, 1), (twos,), 0, 1 << 20) % (margin + 1)
    tallies = tallies.at[1:1 + 2 * twos:2].set(donor - shifted).at[2:2 + 2 * twos:2].set(sink + shifted)
    return tallies[jax.random.permutation(jax.random.fold_in(own_key, 2), number_of)]


def bell_draw(key, shape, deviation, reach, pieces=(), kind=jnp.bfloat16):
    values = jax.random.normal(key, shape, jnp.float32) * deviation
    if len(pieces) > 0:
        values = block_scale(key, shape, pieces, -0.22, 0.18) * values
    return jnp.clip(values, min=-reach, max=reach).astype(kind)


def setup_inputs(seed: int = 0) -> dict:
    arg_keys = jax.random.split(jax.random.key(seed), 12)
    return {
        "query_matrix": bell_draw(arg_keys[0], (PACK_COUNT, PACK_TOKENS, QUERY_HEADS * HEAD_WIDTH), 1.0, 6.0, ((0, 8), (1, 16))),
        "key_matrix": bell_draw(arg_keys[1], (PACK_COUNT, PACK_TOKENS, KEY_VALUE_HEADS * HEAD_WIDTH), 1.0, 6.0, ((0, 8), (1, 16))),
        "value_matrix": bell_draw(arg_keys[2], (PACK_COUNT, PACK_TOKENS, KEY_VALUE_HEADS * HEAD_WIDTH), 1.0, 6.0, ((0, 8), (1, 16))),
        "output_gradient": bell_draw(arg_keys[3], (PACK_COUNT, PACK_TOKENS, QUERY_HEADS * HEAD_WIDTH), 1.0, 6.0, ((0, 8), (1, 16))),
        "log_softmax_norm": jnp.clip(6.0 + 3.0 * jax.random.uniform(arg_keys[4], (PACK_COUNT, QUERY_HEADS, PACK_TOKENS), jnp.float32) ** block_scale(arg_keys[4], (PACK_COUNT, QUERY_HEADS, PACK_TOKENS), ((0, 8), (2, 16)), -0.2, 0.2), 6.0, 9.0),
        "output_dot_rows": bell_draw(arg_keys[5], (PACK_COUNT, QUERY_HEADS, PACK_TOKENS), 8.0, 48.0, ((0, 8), (2, 16)), jnp.float32),
        "shared_prefix_keys": bell_draw(arg_keys[6], (PREFIX_LENGTH, KEY_VALUE_HEADS * HEAD_WIDTH), 1.0, 6.0),
        "shared_prefix_values": bell_draw(arg_keys[7], (PREFIX_LENGTH, KEY_VALUE_HEADS * HEAD_WIDTH), 1.0, 6.0),
        "prefix_len": draw_prefix_len(jax.random.fold_in(arg_keys[11], 71), 0),
        "segments": jax.vmap(lambda own: jnp.searchsorted(jnp.cumsum(ragged_sizes(own, 8, PACK_TOKENS, PACK_TOKENS // 4, 2)), jnp.arange(PACK_TOKENS), side="right"))(jax.random.split(arg_keys[9], PACK_COUNT)).reshape((PACK_COUNT, PACK_TOKENS)).astype(jnp.int32),
        "span_order": jax.vmap(lambda own: jax.random.permutation(own, SPANS))(jax.random.split(arg_keys[10], PACK_COUNT)).reshape((PACK_COUNT, SPANS)).astype(jnp.int32),
    }


def head_grads(query_h, grad_h, norm_h, delta_h, key_h, value_h, visible):
    scale = query_h.shape[-1] ** -0.5
    scores = jnp.dot(query_h, key_h.T, preferred_element_type=jnp.float32) * scale
    probs = jnp.where(visible, jnp.exp(scores - norm_h[:, None]), jnp.zeros_like(scores))
    probs_low = probs.astype(jnp.bfloat16)
    value_gradients = jnp.dot(probs_low.T, grad_h, preferred_element_type=jnp.float32)
    grad_probs = jnp.dot(grad_h, value_h.T, preferred_element_type=jnp.float32)
    grad_scores = (probs * (grad_probs - delta_h[:, None])).astype(jnp.bfloat16)
    grad_query = jnp.dot(grad_scores, key_h, preferred_element_type=jnp.float32) * scale
    key_gradients = jnp.dot(grad_scores.T, query_h, preferred_element_type=jnp.float32) * scale
    return grad_query, key_gradients, value_gradients


def pack_grads(query_matrix, key_matrix, value_matrix, output_gradient, log_softmax_norm, output_dot_rows, shared_prefix_keys, shared_prefix_values, plen, doc_ids, order):
    half = S_DEV // 2
    token_count = query_matrix.shape[0]
    rows = jnp.arange(token_count, dtype=jnp.int32)
    position = order[rows // half] * half + rows % half
    document = doc_ids[position]
    visible = (position[:, None] >= position[None, :]) & (document[:, None] == document[None, :])
    prefix_open = jnp.broadcast_to(jnp.arange(PREFIX_LENGTH, dtype=jnp.int32)[None, :] < plen, (token_count, PREFIX_LENGTH))
    query_group = QUERY_HEADS // KEY_VALUE_HEADS
    query_block = query_matrix.reshape(token_count, QUERY_HEADS, HEAD_WIDTH)
    grads = output_gradient.reshape(token_count, QUERY_HEADS, HEAD_WIDTH)
    every_key = key_matrix.reshape(token_count, KEY_VALUE_HEADS, HEAD_WIDTH)
    every_value = value_matrix.reshape(token_count, KEY_VALUE_HEADS, HEAD_WIDTH)
    leading_keys = shared_prefix_keys.reshape(PREFIX_LENGTH, KEY_VALUE_HEADS, HEAD_WIDTH)
    leading_values = shared_prefix_values.reshape(PREFIX_LENGTH, KEY_VALUE_HEADS, HEAD_WIDTH)

    def one_head(head):
        shared = head // query_group
        query_h = lax.dynamic_index_in_dim(query_block, head, 1, keepdims=False)
        grad_h = lax.dynamic_index_in_dim(grads, head, 1, keepdims=False)
        norm_h = lax.dynamic_index_in_dim(log_softmax_norm, head, 0, keepdims=False)
        delta_h = lax.dynamic_index_in_dim(output_dot_rows, head, 0, keepdims=False)
        key_h = lax.dynamic_index_in_dim(every_key, shared, 1, keepdims=False)
        value_h = lax.dynamic_index_in_dim(every_value, shared, 1, keepdims=False)
        pkey_h = lax.dynamic_index_in_dim(leading_keys, shared, 1, keepdims=False)
        pvalue_h = lax.dynamic_index_in_dim(leading_values, shared, 1, keepdims=False)
        main = head_grads(query_h, grad_h, norm_h, delta_h, key_h, value_h, visible)
        extra = head_grads(query_h, grad_h, norm_h, delta_h, pkey_h, pvalue_h, prefix_open)
        return main[0] + extra[0], main[1], main[2], extra[1], extra[2]

    gq, key_gradient, value_gradient, prefix_key_gradient, prefix_value_gradient = lax.map(one_head, jnp.arange(QUERY_HEADS, dtype=jnp.int32))
    grad_query = jnp.transpose(gq, (1, 0, 2)).reshape(token_count, QUERY_HEADS * HEAD_WIDTH).astype(jnp.bfloat16)
    key_gradients = jnp.transpose(key_gradient.reshape(KEY_VALUE_HEADS, query_group, token_count, HEAD_WIDTH).sum(axis=1), (1, 0, 2)).reshape(token_count, KEY_VALUE_HEADS * HEAD_WIDTH).astype(jnp.bfloat16)
    value_gradients = jnp.transpose(value_gradient.reshape(KEY_VALUE_HEADS, query_group, token_count, HEAD_WIDTH).sum(axis=1), (1, 0, 2)).reshape(token_count, KEY_VALUE_HEADS * HEAD_WIDTH).astype(jnp.bfloat16)
    prefix_key_rows = jnp.transpose(prefix_key_gradient.reshape(KEY_VALUE_HEADS, query_group, PREFIX_LENGTH, HEAD_WIDTH).sum(axis=1), (1, 0, 2)).reshape(PREFIX_LENGTH, KEY_VALUE_HEADS * HEAD_WIDTH)
    prefix_value_rows = jnp.transpose(prefix_value_gradient.reshape(KEY_VALUE_HEADS, query_group, PREFIX_LENGTH, HEAD_WIDTH).sum(axis=1), (1, 0, 2)).reshape(PREFIX_LENGTH, KEY_VALUE_HEADS * HEAD_WIDTH)
    return grad_query, key_gradients, value_gradients, prefix_key_rows, prefix_value_rows


def reference(query_matrix, key_matrix, value_matrix, output_gradient, log_softmax_norm, output_dot_rows, shared_prefix_keys, shared_prefix_values, prefix_len, segments, span_order):
    all_query, all_key, all_value = [], [], []
    prefix_key_rows = jnp.zeros((PREFIX_LENGTH, KEY_VALUE_HEADS * HEAD_WIDTH), jnp.float32)
    prefix_value_rows = jnp.zeros((PREFIX_LENGTH, KEY_VALUE_HEADS * HEAD_WIDTH), jnp.float32)
    for pack in range(PACK_COUNT):
        result = pack_grads(query_matrix[pack], key_matrix[pack], value_matrix[pack], output_gradient[pack], log_softmax_norm[pack], output_dot_rows[pack], shared_prefix_keys, shared_prefix_values, prefix_len[pack], segments[pack], span_order[pack])
        all_query.append(result[0])
        all_key.append(result[1])
        all_value.append(result[2])
        prefix_key_rows = prefix_key_rows + result[3]
        prefix_value_rows = prefix_value_rows + result[4]
    return jnp.stack(all_query), jnp.stack(all_key), jnp.stack(all_value), prefix_key_rows, prefix_value_rows
```

```python
import functools

import jax
import jax.numpy as jnp
from jax import lax
from jax.experimental import pallas as pl
from jax.experimental.pallas import tpu as pltpu
from jax.sharding import PartitionSpec as P

QUERY_HEADS = 32
KEY_VALUE_HEADS = 4
GROUP = QUERY_HEADS // KEY_VALUE_HEADS
WIDTH = 128
SPAN = 96
PREFIX = 256
TOKENS = 3072
SPANS = 32
CHUNK = 256
SCALE = WIDTH**-0.5
LOG2E = 1.4426950408889634
LANES = GROUP * SPAN


def nt(a, b):
    return lax.dot_general(a, b, (((1,), (1,)), ((), ())), preferred_element_type=jnp.float32)


def nn(a, b):
    return lax.dot_general(a, b, (((1,), (0,)), ((), ())), preferred_element_type=jnp.float32)


def tn(a, b):
    return lax.dot_general(a, b, (((0,), (0,)), ((), ())), preferred_element_type=jnp.float32)


def main_kernel(
    heads,
    spans,
    order_ref,
    starts_ref,
    plen_ref,
    place_ref,
    q_ref,
    g_ref,
    norm_ref,
    dot_ref,
    k_ref,
    v_ref,
    pk_ref,
    pv_ref,
    dq_ref,
    dk_ref,
    dv_ref,
    dpk_ref,
    dpv_ref,
    kcat,
    vcat,
    dkacc,
    dvacc,
):
    lane_row = lax.rem(lax.broadcasted_iota(jnp.int32, (1, LANES), 1), SPAN)
    key_row = lax.broadcasted_iota(jnp.int32, (CHUNK, 1), 0)
    prefix_seen = lax.broadcasted_iota(jnp.int32, (PREFIX, 1), 0) < plen_ref[0]

    def head_step(h, _):
        cols = pl.ds(pl.multiple_of(h * WIDTH, WIDTH), WIDTH)
        kcat[:PREFIX] = pk_ref[:, cols]
        vcat[:PREFIX] = pv_ref[:, cols]

        def reorder(t, _):
            src = pl.ds(pl.multiple_of(t * SPAN, SPAN), SPAN)
            dst = pl.ds(pl.multiple_of(PREFIX + order_ref[t] * SPAN, 32), SPAN)
            kcat[dst] = k_ref[src, cols]
            vcat[dst] = v_ref[src, cols]
            return 0

        lax.fori_loop(0, SPANS, reorder, 0)
        dkacc[...] = jnp.zeros_like(dkacc)
        dvacc[...] = jnp.zeros_like(dvacc)

        def span_step(s, _):
            rows = pl.ds(pl.multiple_of(s * SPAN, SPAN), SPAN)

            def heads_of(ref):
                return jnp.concatenate(
                    [
                        ref[rows, pl.ds(pl.multiple_of((h * GROUP + g) * WIDTH, WIDTH), WIDTH)]
                        for g in range(GROUP)
                    ],
                    axis=0,
                )

            q = heads_of(q_ref)
            grad = heads_of(g_ref)
            norm = norm_ref[s, pl.ds(h, 1), :] * LOG2E
            dot = dot_ref[s, pl.ds(h, 1), :]
            place = place_ref[s]
            upper = place * SPAN + lane_row
            lower = jnp.zeros_like(upper)
            first = jnp.int32(0)
            for d in range(8):
                start = starts_ref[d]
                lower = jnp.maximum(lower, jnp.where(start <= upper, start, 0))
                first = jnp.maximum(first, jnp.where(start <= place * SPAN, start, 0))

            def tile(keys, values, seen):
                st = nt(keys, q)
                p = jnp.where(seen, jnp.exp2(st * (SCALE * LOG2E) - norm), 0.0)
                dv = nn(p.astype(jnp.bfloat16), grad)
                dp = nt(values, grad)
                ds = (p * (dp - dot)).astype(jnp.bfloat16)
                dk = nn(ds, q)
                dq = tn(ds, keys)
                return dk, dv, dq

            dk, dv, dq = tile(kcat[:PREFIX], vcat[:PREFIX], prefix_seen)
            dkacc[:PREFIX] += dk
            dvacc[:PREFIX] += dv
            end = (place + 1) * SPAN

            def chunk_step(j, total):
                begin = end - (j + 1) * CHUNK
                at = pl.ds(pl.multiple_of(PREFIX + begin, 32), CHUNK)
                pos = begin + key_row
                seen = (pos >= lower) & (pos <= upper)
                dk, dv, dq = tile(kcat[at], vcat[at], seen)
                dkacc[at] += dk
                dvacc[at] += dv
                return total + dq

            steps = (end - first + CHUNK - 1) // CHUNK
            dq = lax.fori_loop(0, steps, chunk_step, dq)
            dq = (dq * SCALE).astype(jnp.bfloat16)
            for g in range(GROUP):
                dq_ref[rows, pl.ds(pl.multiple_of((h * GROUP + g) * WIDTH, WIDTH), WIDTH)] = dq[
                    g * SPAN : (g + 1) * SPAN
                ]
            return 0

        lax.fori_loop(0, spans, span_step, 0)
        dpk_ref[:, cols] = dkacc[:PREFIX] * SCALE
        dpv_ref[:, cols] = dvacc[:PREFIX]

        def give(t, _):
            dst = pl.ds(pl.multiple_of(t * SPAN, SPAN), SPAN)
            src = pl.ds(pl.multiple_of(PREFIX + order_ref[t] * SPAN, 32), SPAN)
            dk_ref[dst, cols] = (dkacc[src] * SCALE).astype(jnp.bfloat16)
            dv_ref[dst, cols] = dvacc[src].astype(jnp.bfloat16)
            return 0

        lax.fori_loop(0, SPANS, give, 0)
        return 0

    lax.fori_loop(0, heads, head_step, 0)


def run_main(heads, spans, order, starts, plen, place, q, g, norm, dot, k, v, pk, pv):
    smem = pl.BlockSpec(memory_space=pltpu.SMEM)
    vmem = pl.BlockSpec(memory_space=pltpu.VMEM)
    return pl.pallas_call(
        functools.partial(main_kernel, heads, spans),
        out_shape=(
            jax.ShapeDtypeStruct(q.shape, jnp.bfloat16),
            jax.ShapeDtypeStruct((TOKENS, heads * WIDTH), jnp.bfloat16),
            jax.ShapeDtypeStruct((TOKENS, heads * WIDTH), jnp.bfloat16),
            jax.ShapeDtypeStruct((PREFIX, heads * WIDTH), jnp.float32),
            jax.ShapeDtypeStruct((PREFIX, heads * WIDTH), jnp.float32),
        ),
        in_specs=[smem] * 4 + [vmem] * 8,
        out_specs=(vmem,) * 5,
        scratch_shapes=[
            pltpu.VMEM((PREFIX + TOKENS, WIDTH), jnp.bfloat16),
            pltpu.VMEM((PREFIX + TOKENS, WIDTH), jnp.bfloat16),
            pltpu.VMEM((PREFIX + TOKENS, WIDTH), jnp.float32),
            pltpu.VMEM((PREFIX + TOKENS, WIDTH), jnp.float32),
        ],
        compiler_params=pltpu.CompilerParams(vmem_limit_bytes=48 * 1024 * 1024),
    )(order, starts, plen, place, q, g, norm, dot, k, v, pk, pv)


def rows_by_span(table, heads):
    spans = table.shape[-1] // SPAN
    return (
        table.reshape(heads, GROUP, spans, SPAN).transpose(2, 0, 1, 3).reshape(spans, heads, LANES)
    )


def local(
    query_matrix,
    key_matrix,
    value_matrix,
    output_gradient,
    log_softmax_norm,
    output_dot_rows,
    shared_prefix_keys,
    shared_prefix_values,
    prefix_len,
    segments,
    span_order,
):
    order = span_order[0]
    own = lax.axis_index("blk")
    starts = jnp.sum(
        segments[0][None, :] < jnp.arange(8, dtype=jnp.int32)[:, None], axis=1, dtype=jnp.int32
    )
    place = lax.dynamic_slice(order, (2 * own,), (2,))
    keys = lax.all_gather(key_matrix[0], "blk", axis=0, tiled=True)
    values = lax.all_gather(value_matrix[0], "blk", axis=0, tiled=True)
    dq, dk, dv, dpk, dpv = run_main(
        KEY_VALUE_HEADS,
        2,
        order,
        starts,
        prefix_len,
        place,
        query_matrix[0],
        output_gradient[0],
        rows_by_span(log_softmax_norm[0], KEY_VALUE_HEADS),
        rows_by_span(output_dot_rows[0], KEY_VALUE_HEADS),
        keys,
        values,
        shared_prefix_keys,
        shared_prefix_values,
    )
    dk = lax.psum_scatter(dk, "blk", scatter_dimension=0, tiled=True)
    dv = lax.psum_scatter(dv, "blk", scatter_dimension=0, tiled=True)
    prefix = lax.psum(jnp.stack([dpk, dpv]), ("dp", "blk"))
    return dq[None], dk[None], dv[None], prefix[0], prefix[1]


def solution(mesh):
    return jax.shard_map(
        local,
        mesh=mesh,
        in_specs=(
            P("dp", "blk", None),
            P("dp", "blk", None),
            P("dp", "blk", None),
            P("dp", "blk", None),
            P("dp", None, "blk"),
            P("dp", None, "blk"),
            P(),
            P(),
            P("dp"),
            P("dp", None),
            P("dp", None),
        ),
        out_specs=(P("dp", "blk", None), P("dp", "blk", None), P("dp", "blk", None), P(), P()),
        check_vma=False,
    )
```

```python
import functools

import jax
import jax.numpy as jnp
from jax import lax
from jax.experimental import pallas as pl
from jax.experimental.pallas import tpu as pltpu
from jax.sharding import PartitionSpec as P

QUERY_HEADS = 32
KEY_VALUE_HEADS = 4
GROUP = QUERY_HEADS // KEY_VALUE_HEADS
WIDTH = 128
SPAN = 96
ROWS = 192
PREFIX = 256
TOKENS = 3072
SPANS = 32
CHUNK = 256
HEADS = 2
HALF = HEADS * GROUP * WIDTH
SCALE = WIDTH**-0.5
LOG2E = 1.4426950408889634
LANES = GROUP * SPAN
MESH = pl.DeviceIdType.MESH
BF16 = jnp.bfloat16
F32 = jnp.float32


def nt(a, b):
    return lax.dot_general(a, b, (((1,), (1,)), ((), ())), preferred_element_type=F32)


def nn(a, b):
    return lax.dot_general(a, b, (((1,), (0,)), ((), ())), preferred_element_type=F32)


def tn(a, b):
    return lax.dot_general(a, b, (((0,), (0,)), ((), ())), preferred_element_type=F32)


class Place:
    def __init__(self):
        self.dp, self.blk = lax.axis_index("dp"), lax.axis_index("blk")
        self.x_lo, self.z = self.dp // 4, lax.rem(self.dp, 4)
        self.y, self.x_hi = self.blk // 4, lax.rem(self.blk // 2, 2)
        self.core = lax.rem(self.blk, 2)
        self.x = self.x_hi * 2 + self.x_lo

    def at(self, dx=0, dy=0, dz=0, other=False):
        x = lax.rem(self.x + dx, 4)
        y = lax.rem(self.y + dy, 4)
        z = lax.rem(self.z + dz, 4)
        core = 1 - self.core if other else self.core
        return (lax.rem(x, 2) * 4 + z, (y * 2 + x // 2) * 2 + core)

    def chip(self, dy, col):
        x_hi = self.x_hi if col == 0 else 1 - self.x_hi
        return lax.rem(self.y + dy, 4) * 2 + x_hi


def meet(peers):
    barrier = pltpu.get_barrier_semaphore()
    for peer in peers:
        pl.semaphore_signal(barrier, inc=1, device_id=peer, device_id_type=MESH)
    pl.semaphore_wait(barrier, len(peers))


def remote(src, dst, send, recv, peer):
    return pltpu.make_async_remote_copy(
        src_ref=src, dst_ref=dst, send_sem=send, recv_sem=recv, device_id=peer, device_id_type=MESH
    )


def lanes(start, size):
    return pl.ds(pl.multiple_of(start, WIDTH), size)


def gather_kernel(
    q_ref,
    g_ref,
    norm_ref,
    dot_ref,
    k_ref,
    v_ref,
    qs_ref,
    gs_ref,
    norms_ref,
    dots_ref,
    kv_ref,
    local_sem,
    pair_send,
    pair_recv,
    swap_send,
    swap_recv,
    y_send,
    y_recv,
    f_send,
    f_recv,
    x_send,
    x_recv,
):
    me = Place()
    core, other = me.core, 1 - me.core
    mine = me.chip(0, 0)
    sources = (k_ref, v_ref)
    own = []
    for h in range(HEADS):
        for i in range(2):
            copy = pltpu.make_async_copy(
                sources[i].at[:, lanes((core * 2 + h) * WIDTH, WIDTH)],
                kv_ref.at[mine, core, h, i],
                local_sem.at[h, i],
            )
            copy.start()
            own.append(copy)
    sibling = me.at(other=True)
    up, down, across = me.at(dy=1), me.at(dy=3), me.at(dx=2)
    meet((sibling, up, down, across))
    sent = []

    def start(copy):
        copy.start()
        sent.append(copy)
        return copy

    pair = [
        [
            start(
                remote(
                    sources[i].at[:, lanes((other * 2 + h) * WIDTH, WIDTH)],
                    kv_ref.at[mine, core, h, i],
                    pair_send.at[h, i],
                    pair_recv.at[h, i],
                    sibling,
                )
            )
            for i in range(2)
        ]
        for h in range(HEADS)
    ]
    swaps = []
    rows16 = pl.ds(pl.multiple_of(other * 16, 16), 16)
    for n, (src, dst) in enumerate(
        (
            (q_ref.at[:, lanes(other * HALF, HALF)], qs_ref),
            (g_ref.at[:, lanes(other * HALF, HALF)], gs_ref),
            (norm_ref.at[rows16], norms_ref),
            (dot_ref.at[rows16], dots_ref),
        )
    ):
        swaps.append(remote(src, dst, swap_send.at[n], swap_recv.at[n], sibling))
    for copy in own:
        copy.wait()

    def y_pair(col, rr, h, r):
        block = kv_ref.at[me.chip(0, col), r, h]
        return [
            start(remote(block, block, y_send.at[d, col, rr, h], y_recv.at[d, col, rr, h], peer))
            for d, peer in enumerate((up, down))
        ]

    y_copies, x_copies, f_copies = {}, {}, {}
    for h in range(HEADS):
        for rr, r in enumerate((core, other)):
            if rr == 1:
                for i in range(2):
                    pair[h][i].wait_recv()
            block = kv_ref.at[mine, r, h]
            x_copies[rr, h] = start(
                remote(block, block, x_send.at[rr, h], x_recv.at[rr, h], across)
            )
            y_copies[0, rr, h] = y_pair(0, rr, h, r)
    for copy in swaps:
        start(copy)

    def forward(col, h):
        for d, (rr, dy, peer) in enumerate(((0, 3, up), (1, 1, down))):
            y_copies[col, rr, h][d].wait_recv()
            block = kv_ref.at[me.chip(dy, col), core if rr == 0 else other, h]
            f_copies[d, col, h] = start(
                remote(block, block, f_send.at[d, col, h], f_recv.at[d, col, h], peer)
            )

    for h in range(HEADS):
        for rr, r in enumerate((core, other)):
            x_copies[rr, h].wait_recv()
            y_copies[1, rr, h] = y_pair(1, rr, h, r)
        forward(0, h)
    for h in range(HEADS):
        forward(1, h)
    for col in range(2):
        for h in range(HEADS):
            y_copies[col, 1, h][0].wait_recv()
            y_copies[col, 0, h][1].wait_recv()
            f_copies[0, col, h].wait_recv()
            f_copies[1, col, h].wait_recv()
    for copy in swaps:
        copy.wait_recv()
    for copy in sent:
        copy.wait_send()


def gather(q, g, norm, dot, k, v):
    dma = pltpu.SemaphoreType.DMA
    anywhere = pl.BlockSpec(memory_space=pl.ANY)
    return pl.pallas_call(
        gather_kernel,
        out_shape=(
            jax.ShapeDtypeStruct((ROWS, HALF), BF16),
            jax.ShapeDtypeStruct((ROWS, HALF), BF16),
            jax.ShapeDtypeStruct((16, ROWS), F32),
            jax.ShapeDtypeStruct((16, ROWS), F32),
            jax.ShapeDtypeStruct((8, 2, HEADS, 2, ROWS, WIDTH), BF16),
        ),
        in_specs=[anywhere] * 6,
        out_specs=(anywhere,) * 5,
        scratch_shapes=[
            dma((HEADS, 2)),
            dma((HEADS, 2)),
            dma((HEADS, 2)),
            dma((4,)),
            dma((4,)),
            dma((2, 2, 2, HEADS)),
            dma((2, 2, 2, HEADS)),
            dma((2, 2, HEADS)),
            dma((2, 2, HEADS)),
            dma((2, HEADS)),
            dma((2, HEADS)),
        ],
        compiler_params=pltpu.CompilerParams(collective_id=0, has_side_effects=True),
        name="gather_keys",
    )(q, g, norm, dot, k, v)


def main_kernel(
    order_ref,
    starts_ref,
    plen_ref,
    q_hbm,
    g_hbm,
    qs_hbm,
    gs_hbm,
    norm_ref,
    norms_ref,
    dot_ref,
    dots_ref,
    kv_ref,
    pk_ref,
    pv_ref,
    dq_ref,
    part_ref,
    dp_ref,
    q_ref,
    g_ref,
    kcat,
    vcat,
    dkacc,
    dvacc,
    sem,
):
    blk = lax.axis_index("blk")
    core = lax.rem(blk, 2)
    chip = blk // 2
    half = lanes(core * HALF, HALF)
    copies = [
        pltpu.make_async_copy(src, dst, sem.at[n])
        for n, (src, dst) in enumerate(
            (
                (q_hbm.at[:, half], q_ref.at[0]),
                (g_hbm.at[:, half], g_ref.at[0]),
                (qs_hbm, q_ref.at[1]),
                (gs_hbm, g_ref.at[1]),
            )
        )
    ]
    for copy in copies:
        copy.start()
    lane_row = lax.rem(lax.broadcasted_iota(jnp.int32, (1, LANES), 1), SPAN)
    key_row = lax.broadcasted_iota(jnp.int32, (CHUNK, 1), 0)
    prefix_seen = lax.broadcasted_iota(jnp.int32, (PREFIX, 1), 0) < plen_ref[0]

    for copy in copies:
        copy.wait()

    for h in range(HEADS):
        cols = lanes((core * 2 + h) * WIDTH, WIDTH)
        kcat[:PREFIX] = pk_ref[:, cols]
        vcat[:PREFIX] = pv_ref[:, cols]

        def reorder(b, _):
            for half_at in range(2):
                dst = pl.ds(
                    pl.multiple_of(PREFIX + order_ref[2 * b + half_at] * SPAN, 32), SPAN
                )
                rows = pl.ds(half_at * SPAN, SPAN)
                kcat[dst] = kv_ref[b // 2, lax.rem(b, 2), h, 0, rows]
                vcat[dst] = kv_ref[b // 2, lax.rem(b, 2), h, 1, rows]
            return 0

        lax.fori_loop(0, SPANS // 2, reorder, 0)
        dkacc[...] = jnp.zeros_like(dkacc)
        dvacc[...] = jnp.zeros_like(dvacc)

        for s in range(4):
            w, r = s // 2, (s % 2) * SPAN
            rows = pl.ds(r, SPAN)

            def heads_of(ref):
                return jnp.concatenate(
                    [ref[w, rows, pl.ds((h * GROUP + g) * WIDTH, WIDTH)] for g in range(GROUP)],
                    axis=0,
                )

            def row_of(own_ref, other_ref):
                if w == 0:
                    at = pl.ds(pl.multiple_of((core * 2 + h) * GROUP, GROUP), GROUP)
                    table = own_ref[at, :][:, r : r + SPAN]
                else:
                    table = other_ref[h * GROUP : (h + 1) * GROUP, r : r + SPAN]
                return jnp.concatenate([table[g : g + 1] for g in range(GROUP)], axis=1)

            q = heads_of(q_ref)
            grad = heads_of(g_ref)
            norm = row_of(norm_ref, norms_ref) * LOG2E
            dot = row_of(dot_ref, dots_ref)
            owner = core if w == 0 else 1 - core
            place = order_ref[chip * 4 + owner * 2 + s % 2]
            upper = place * SPAN + lane_row
            lower = jnp.zeros_like(upper)
            first = jnp.int32(0)
            for d in range(8):
                start = starts_ref[d]
                lower = jnp.maximum(lower, jnp.where(start <= upper, start, 0))
                first = jnp.maximum(first, jnp.where(start <= place * SPAN, start, 0))

            def tile(keys, values, seen):
                st = nt(keys, q)
                p = jnp.where(seen, jnp.exp2(st * (SCALE * LOG2E) - norm), 0.0)
                dv = nn(p.astype(BF16), grad)
                dp = nt(values, grad)
                ds = (p * (dp - dot)).astype(BF16)
                dk = nn(ds, q)
                dq = tn(ds, keys)
                return dk, dv, dq

            dk, dv, dq = tile(kcat[:PREFIX], vcat[:PREFIX], prefix_seen)
            dkacc[:PREFIX] += dk
            dvacc[:PREFIX] += dv
            end = (place + 1) * SPAN

            def chunk_step(j, total):
                begin = end - (j + 1) * CHUNK
                at = pl.ds(pl.multiple_of(PREFIX + begin, 32), CHUNK)
                pos = begin + key_row
                seen = (pos >= lower) & (pos <= upper)
                dk, dv, dq = tile(kcat[at], vcat[at], seen)
                dkacc[at] += dk
                dvacc[at] += dv
                return total + dq

            steps = (end - first + CHUNK - 1) // CHUNK
            dq = lax.fori_loop(0, steps, chunk_step, dq)
            dq = (dq * SCALE).astype(BF16)
            for g in range(GROUP):
                dq_ref[w, rows, pl.ds((h * GROUP + g) * WIDTH, WIDTH)] = dq[
                    g * SPAN : (g + 1) * SPAN
                ]
        dp_ref[0, :, h * WIDTH : (h + 1) * WIDTH] = dkacc[:PREFIX] * SCALE
        dp_ref[1, :, h * WIDTH : (h + 1) * WIDTH] = dvacc[:PREFIX]

        def give(b, _):
            for half_at in range(2):
                src = pl.ds(
                    pl.multiple_of(PREFIX + order_ref[2 * b + half_at] * SPAN, 32), SPAN
                )
                rows = pl.ds(half_at * SPAN, SPAN)
                part_ref[b // 2, lax.rem(b, 2), h, 0, rows] = (dkacc[src] * SCALE).astype(BF16)
                part_ref[b // 2, lax.rem(b, 2), h, 1, rows] = dvacc[src].astype(BF16)
            return 0

        lax.fori_loop(0, SPANS // 2, give, 0)


def run_main(order, starts, plen, q, g, qs, gs, norm, norms, dot, dots, kv, pk, pv):
    smem = pl.BlockSpec(memory_space=pltpu.SMEM)
    vmem = pl.BlockSpec(memory_space=pltpu.VMEM)
    anywhere = pl.BlockSpec(memory_space=pl.ANY)
    return pl.pallas_call(
        main_kernel,
        out_shape=(
            jax.ShapeDtypeStruct((2, ROWS, HALF), BF16),
            jax.ShapeDtypeStruct((8, 2, HEADS, 2, ROWS, WIDTH), BF16),
            jax.ShapeDtypeStruct((2, PREFIX, HEADS * WIDTH), F32),
        ),
        in_specs=[smem] * 3 + [anywhere] * 4 + [vmem] * 7,
        out_specs=(vmem,) * 3,
        scratch_shapes=[
            pltpu.VMEM((2, ROWS, HALF), BF16),
            pltpu.VMEM((2, ROWS, HALF), BF16),
            pltpu.VMEM((PREFIX + TOKENS, WIDTH), BF16),
            pltpu.VMEM((PREFIX + TOKENS, WIDTH), BF16),
            pltpu.VMEM((PREFIX + TOKENS, WIDTH), F32),
            pltpu.VMEM((PREFIX + TOKENS, WIDTH), F32),
            pltpu.SemaphoreType.DMA((4,)),
        ],
        compiler_params=pltpu.CompilerParams(vmem_limit_bytes=48 * 1024 * 1024),
        name="tiles",
    )(order, starts, plen, q, g, qs, gs, norm, norms, dot, dots, kv, pk, pv)


def reduce_kernel(
    dq_in,
    part_ref,
    dp_ref,
    dq_ref,
    dk_ref,
    dv_ref,
    dpk_ref,
    dpv_ref,
    a_buf,
    b_buf,
    c_buf,
    c_out,
    x_buf,
    x_out,
    held,
    last_out,
    last_buf,
    z_buf,
    z_sum,
    px_buf,
    px_sum,
    py_buf,
    fin,
    fin_other,
    dq_sem,
    a_sem,
    b_sem,
    c_sem,
    x_sem,
    last_sem,
    z_sem,
    px_sem,
    py_sem,
    gx_sem,
    gz_sem,
    gc_sem,
):
    me = Place()
    core, other = me.core, 1 - me.core
    sibling = me.at(other=True)
    up, down, across = me.at(dy=1), me.at(dy=3), me.at(dx=2)
    half = lanes(core * HALF, HALF)
    keep = pltpu.make_async_copy(dq_in.at[0], dq_ref.at[:, half], dq_sem.at[2])
    keep.start()
    z_peers = [me.at(dz=d) for d in (1, 2, 3)]
    x_peers = [me.at(dx=d) for d in (1, 2, 3)]
    y_peers = [me.at(dy=d) for d in (1, 2, 3)]
    meet([sibling] + z_peers + x_peers + y_peers)
    sent = []

    def start(src, dst, sem, peer):
        copy = remote(src, dst, sem.at[0], sem.at[1], peer)
        copy.start()
        sent.append(copy)
        return copy

    far, near, mid = {}, {}, {}
    for h in range(HEADS):
        for col in (1, 0):
            for d, peer in enumerate((up, down)):
                r = 1 - d
                far[d, col, h] = start(
                    part_ref.at[me.chip(2, col), r, h],
                    a_buf.at[d, col, h],
                    a_sem.at[d, col, h],
                    peer,
                )
        for col in (1, 0):
            for d, (peer, dy) in enumerate(((up, 1), (down, 3))):
                near[d, col, h] = start(
                    part_ref.at[me.chip(dy, col), d, h],
                    b_buf.at[d, col, h],
                    b_sem.at[d, col, h],
                    peer,
                )
    z_copies = [
        start(
            dp_ref.at[:, pl.ds(pl.multiple_of(lax.rem(me.z + n + 1, 4) * 64, 64), 64)],
            z_buf.at[n],
            z_sem.at[n],
            z_peers[n],
        )
        for n in range(3)
    ]
    back = start(dq_in.at[1], dq_ref.at[:, half], dq_sem, sibling)

    def pass_on(h, col):
        for d, (peer, dy) in enumerate(((up, 1), (down, 3))):
            r = 1 - d
            far[d, col, h].wait_recv()
            c_out[d, col, h] = (
                part_ref[me.chip(dy, col), r, h].astype(F32) + a_buf[d, col, h].astype(F32)
            ).astype(BF16)
            mid[d, col, h] = start(
                c_out.at[d, col, h], c_buf.at[d, col, h], c_sem.at[d, col, h], peer
            )

    def column_sum(h, col, r):
        d = 1 - r
        mid[d, col, h].wait_recv()
        near[1 - d, col, h].wait_recv()
        return (
            part_ref[me.chip(0, col), r, h].astype(F32)
            + c_buf[d, col, h].astype(F32)
            + b_buf[1 - d, col, h].astype(F32)
        )

    x_copies = {}
    pass_on(0, 1)
    pass_on(0, 0)
    for copy in z_copies:
        copy.wait_recv()
    z_sum[...] = (
        dp_ref[:, pl.ds(pl.multiple_of(me.z * 64, 64), 64)] + z_buf[0] + z_buf[1] + z_buf[2]
    )
    px_copies = [
        start(
            z_sum.at[:, pl.ds(pl.multiple_of(lax.rem(me.x + n + 1, 4) * 16, 16), 16)],
            px_buf.at[n],
            px_sem.at[n],
            x_peers[n],
        )
        for n in range(3)
    ]
    pass_on(1, 1)
    pass_on(1, 0)

    def over_x(h):
        for r in range(2):
            x_out[r, h] = column_sum(h, 1, r).astype(BF16)
            x_copies[r, h] = start(x_out.at[r, h], x_buf.at[r, h], x_sem.at[r, h], across)

    over_x(0)
    for copy in px_copies:
        copy.wait_recv()
    piece = (
        z_sum[:, pl.ds(pl.multiple_of(me.x * 16, 16), 16)] + px_buf[0] + px_buf[1] + px_buf[2]
    )
    px_sum[...] = piece
    py_buf[me.y] = piece
    py_copies = [
        start(px_sum, py_buf.at[me.y], py_sem.at[n], y_peers[n]) for n in range(3)
    ]
    over_x(1)
    for h in range(HEADS):
        for r in range(2):
            held[r, h] = column_sum(h, 0, r)
    for copy in py_copies:
        copy.wait_recv()
    fin[me.z, me.x] = ((py_buf[0] + py_buf[1]) + py_buf[2]) + py_buf[3]
    gx_copies = [
        start(fin.at[me.z, me.x], fin.at[me.z, me.x], gx_sem.at[n], x_peers[n]) for n in range(3)
    ]
    last = {}
    for h in range(HEADS):
        for r in range(2):
            x_copies[r, h].wait_recv()
        for i in range(2):
            last_out[h, i] = (
                held[other, h, i] + x_buf[other, h, i].astype(F32)
            ).astype(BF16)
        last[h] = start(last_out.at[h], last_buf.at[h], last_sem.at[h], sibling)
    for copy in gx_copies:
        copy.wait_recv()
    gz_copies = [start(fin.at[me.z], fin.at[me.z], gz_sem.at[n], z_peers[n]) for n in range(3)]
    for h in range(HEADS):
        for i, ref in enumerate((dk_ref, dv_ref)):
            ref[:, lanes((core * 2 + h) * WIDTH, WIDTH)] = (
                held[core, h, i] + x_buf[core, h, i].astype(F32)
            ).astype(BF16)
    for copy in gz_copies:
        copy.wait_recv()
    whole = start(fin, fin_other, gc_sem, sibling)
    for h in range(HEADS):
        last[h].wait_recv()
        for i, ref in enumerate((dk_ref, dv_ref)):
            ref[:, lanes((other * 2 + h) * WIDTH, WIDTH)] = last_buf[h, i]

    def lay(src, which):
        at = lanes(which * HEADS * WIDTH, HEADS * WIDTH)
        for z in range(4):
            for x in range(4):
                rows = pl.ds(z * 64 + x * 16, 16)
                dpk_ref[rows, at] = src[z, x, 0]
                dpv_ref[rows, at] = src[z, x, 1]

    lay(fin, core)
    whole.wait_recv()
    lay(fin_other, other)
    back.wait_recv()
    keep.wait()
    for copy in sent:
        copy.wait_send()


def reduce(dq, part, dp):
    vmem = pl.BlockSpec(memory_space=pltpu.VMEM)
    anywhere = pl.BlockSpec(memory_space=pl.ANY)
    dma = pltpu.SemaphoreType.DMA
    unit = (2, ROWS, WIDTH)
    wide = HEADS * WIDTH
    return pl.pallas_call(
        reduce_kernel,
        out_shape=(
            jax.ShapeDtypeStruct((ROWS, 2 * HALF), BF16),
            jax.ShapeDtypeStruct((ROWS, 2 * wide), BF16),
            jax.ShapeDtypeStruct((ROWS, 2 * wide), BF16),
            jax.ShapeDtypeStruct((PREFIX, 2 * wide), F32),
            jax.ShapeDtypeStruct((PREFIX, 2 * wide), F32),
        ),
        in_specs=[anywhere, vmem, vmem],
        out_specs=(anywhere, vmem, vmem, vmem, vmem),
        scratch_shapes=[
            pltpu.VMEM((2, 2, HEADS) + unit, BF16),
            pltpu.VMEM((2, 2, HEADS) + unit, BF16),
            pltpu.VMEM((2, 2, HEADS) + unit, BF16),
            pltpu.VMEM((2, 2, HEADS) + unit, BF16),
            pltpu.VMEM((2, HEADS) + unit, BF16),
            pltpu.VMEM((2, HEADS) + unit, BF16),
            pltpu.VMEM((2, HEADS) + unit, F32),
            pltpu.VMEM((HEADS,) + unit, BF16),
            pltpu.VMEM((HEADS,) + unit, BF16),
            pltpu.VMEM((3, 2, 64, wide), F32),
            pltpu.VMEM((2, 64, wide), F32),
            pltpu.VMEM((3, 2, 16, wide), F32),
            pltpu.VMEM((2, 16, wide), F32),
            pltpu.VMEM((4, 2, 16, wide), F32),
            pltpu.VMEM((4, 4, 2, 16, wide), F32),
            pltpu.VMEM((4, 4, 2, 16, wide), F32),
            dma((3,)),
            dma((2, 2, HEADS, 2)),
            dma((2, 2, HEADS, 2)),
            dma((2, 2, HEADS, 2)),
            dma((2, HEADS, 2)),
            dma((HEADS, 2)),
            dma((3, 2)),
            dma((3, 2)),
            dma((3, 2)),
            dma((3, 2)),
            dma((3, 2)),
            dma((2,)),
        ],
        compiler_params=pltpu.CompilerParams(
            collective_id=1, has_side_effects=True, vmem_limit_bytes=40 * 1024 * 1024
        ),
        name="reduce_sums",
    )(dq, part, dp)


def local(
    query_matrix,
    key_matrix,
    value_matrix,
    output_gradient,
    log_softmax_norm,
    output_dot_rows,
    shared_prefix_keys,
    shared_prefix_values,
    prefix_len,
    segments,
    span_order,
):
    order = span_order[0]
    starts = jnp.sum(
        segments[0][None, :] < jnp.arange(8, dtype=jnp.int32)[:, None], axis=1, dtype=jnp.int32
    )
    q, g, norm, dot = query_matrix[0], output_gradient[0], log_softmax_norm[0], output_dot_rows[0]
    qs, gs, norms, dots, kv = gather(q, g, norm, dot, key_matrix[0], value_matrix[0])
    dq, part, dp = run_main(
        order,
        starts,
        prefix_len,
        q,
        g,
        qs,
        gs,
        norm,
        norms,
        dot,
        dots,
        kv,
        shared_prefix_keys,
        shared_prefix_values,
    )
    dq, dk, dv, dpk, dpv = reduce(dq, part, dp)
    return dq[None], dk[None], dv[None], dpk, dpv


def solution(mesh):
    return jax.shard_map(
        local,
        mesh=mesh,
        in_specs=(
            P("dp", "blk", None),
            P("dp", "blk", None),
            P("dp", "blk", None),
            P("dp", "blk", None),
            P("dp", None, "blk"),
            P("dp", None, "blk"),
            P(),
            P(),
            P("dp"),
            P("dp", None),
            P("dp", None),
        ),
        out_specs=(P("dp", "blk", None), P("dp", "blk", None), P("dp", "blk", None), P(), P()),
        check_vma=False,
    )
```

```python
import functools

import jax
import jax.numpy as jnp
from jax import lax
from jax.experimental import pallas as pl
from jax.experimental.pallas import tpu as pltpu
from jax.sharding import PartitionSpec as P

QUERY_HEADS = 32
KEY_VALUE_HEADS = 4
GROUP = QUERY_HEADS // KEY_VALUE_HEADS
WIDTH = 128
SPAN = 96
ROWS = 192
PREFIX = 256
TOKENS = 3072
SPANS = 32
BACK = 8
REACH = BACK + 1
STARTS, PLACES, BLOCKS, HALVES, SLOTS = 0, 8, 16, 64, 128
HEADS = 2
UNITS = 2 * HEADS
HALF = HEADS * GROUP * WIDTH
SCALE = WIDTH**-0.5
LOG2E = 1.4426950408889634
LANES = GROUP * SPAN
MESH = pl.DeviceIdType.MESH
BF16 = jnp.bfloat16
F32 = jnp.float32


def nt(a, b):
    return lax.dot_general(a, b, (((1,), (1,)), ((), ())), preferred_element_type=F32)


def nn(a, b):
    return lax.dot_general(a, b, (((1,), (0,)), ((), ())), preferred_element_type=F32)


def tn(a, b):
    return lax.dot_general(a, b, (((0,), (0,)), ((), ())), preferred_element_type=F32)


class Place:
    def __init__(self):
        self.dp, self.blk = lax.axis_index("dp"), lax.axis_index("blk")
        self.x_lo, self.z = self.dp // 4, lax.rem(self.dp, 4)
        self.y, self.x_hi = self.blk // 4, lax.rem(self.blk // 2, 2)
        self.core = lax.rem(self.blk, 2)
        self.x = self.x_hi * 2 + self.x_lo

    def at(self, dx=0, dy=0, dz=0, other=False):
        x = lax.rem(self.x + dx, 4)
        y = lax.rem(self.y + dy, 4)
        z = lax.rem(self.z + dz, 4)
        core = 1 - self.core if other else self.core
        return (lax.rem(x, 2) * 4 + z, (y * 2 + x // 2) * 2 + core)

    def chip(self, dy, col):
        x_hi = self.x_hi if col == 0 else 1 - self.x_hi
        return lax.rem(self.y + dy, 4) * 2 + x_hi


def meet(peers):
    barrier = pltpu.get_barrier_semaphore()
    for peer in peers:
        pl.semaphore_signal(barrier, inc=1, device_id=peer, device_id_type=MESH)
    pl.semaphore_wait(barrier, len(peers))


def remote(src, dst, send, recv, peer):
    return pltpu.make_async_remote_copy(
        src_ref=src, dst_ref=dst, send_sem=send, recv_sem=recv, device_id=peer, device_id_type=MESH
    )


def lanes(start, size):
    return pl.ds(pl.multiple_of(start, WIDTH), size)


def prepare_kernel(order_ref, segments_ref, out_ref, inverse):
    mine = lax.axis_index("blk") // 2
    core = lax.rem(lax.axis_index("blk"), 2)
    segments = segments_ref[...]
    out_ref[STARTS] = 0
    for d in range(1, 8):
        out_ref[STARTS + d] = jnp.sum((segments < d).astype(jnp.int32))
    for t in range(SPANS):
        inverse[order_ref[t]] = t
    places = []
    for s in range(4):
        place = order_ref[mine * 4 + (core if s < 2 else 1 - core) * 2 + s % 2]
        places.append(place)
        out_ref[PLACES + s] = place
        for n in range(REACH):
            t = inverse[jnp.maximum(place - BACK + n, 0)]
            out_ref[BLOCKS + s * REACH + n] = lax.shift_right_logical(t, 1)
            out_ref[HALVES + s * REACH + n] = t & 1
    for t in range(SPANS):
        there = order_ref[t]
        for s in range(4):
            at = there - places[s] + BACK
            out_ref[SLOTS + t * 4 + s] = jnp.where((at >= 0) & (at <= BACK), at, REACH)


def prepare(order, segments):
    smem = pl.BlockSpec(memory_space=pltpu.SMEM)
    return pl.pallas_call(
        prepare_kernel,
        out_shape=jax.ShapeDtypeStruct((256,), jnp.int32),
        in_specs=[smem, pl.BlockSpec(memory_space=pltpu.VMEM)],
        out_specs=smem,
        scratch_shapes=[pltpu.SMEM((SPANS,), jnp.int32)],
        name="tables",
    )(order, segments)


def fused_kernel(
    index_ref,
    plen_ref,
    q_hbm,
    g_hbm,
    norm_hbm,
    dot_hbm,
    k_hbm,
    v_hbm,
    pk_hbm,
    pv_hbm,
    dq_ref,
    dk_ref,
    dv_ref,
    dpk_ref,
    dpv_ref,
    q_ref,
    g_ref,
    table,
    prefix,
    kv_0,
    kv_1,
    kv_2,
    kv_3,
    window,
    probs,
    slots_0,
    slots_1,
    dq_prefix,
    dq_stage,
    dp_ref,
    far_out,
    near_out,
    edge_out,
    xf_out,
    a_buf,
    b_buf,
    e_buf,
    c_buf,
    c_out,
    x_buf,
    x_out,
    xf_buf,
    held,
    last_out,
    last_buf,
    z_buf,
    z_sum,
    px_buf,
    px_sum,
    py_buf,
    fin,
    fin_other,
    load_sem,
    own_sem,
    pair_sem,
    swap_sem,
    y_sem,
    f_sem,
    gx_sem,
    gf_sem,
    keep_sem,
    back_sem,
    a_sem,
    b_sem,
    e_sem,
    c_sem,
    x_sem,
    xf_sem,
    last_sem,
    z_sem,
    px_sem,
    py_sem,
    ax_sem,
    az_sem,
    ac_sem,
):
    me = Place()
    core, other = me.core, 1 - me.core
    mine = me.chip(0, 0)
    sibling = me.at(other=True)
    up, down, across = me.at(dy=1), me.at(dy=3), me.at(dx=2)
    z_peers = [me.at(dz=d) for d in (1, 2, 3)]
    x_peers = [me.at(dx=d) for d in (1, 2, 3)]
    y_peers = [me.at(dy=d) for d in (1, 2, 3)]
    half = lanes(core * HALF, HALF)
    wide = HEADS * WIDTH
    sources, kv, slots = (k_hbm, v_hbm), (kv_0, kv_1, kv_2, kv_3), (slots_0, slots_1)
    sent = []

    def start(src, dst, sem, peer):
        copy = remote(src, dst, sem.at[0], sem.at[1], peer)
        copy.start()
        sent.append(copy)
        return copy

    def fetch(src, dst, sem):
        copy = pltpu.make_async_copy(src, dst, sem)
        copy.start()
        return copy

    def columns(u, which):
        return sources[u % 2].at[:, :, lanes((which * 2 + u // 2) * WIDTH, WIDTH)]

    own = [
        fetch(columns(u, core), kv[u].at[mine * 2 + core], own_sem.at[u]) for u in range(UNITS)
    ]
    rows16 = pl.ds(pl.multiple_of(core * 16, 16), 16)
    other16 = pl.ds(pl.multiple_of(other * 16, 16), 16)
    loads = [
        fetch(src, dst, load_sem.at[n])
        for n, (src, dst) in enumerate(
            (
                (q_hbm.at[:, half], q_ref.at[0]),
                (g_hbm.at[:, half], g_ref.at[0]),
                (norm_hbm.at[rows16], table.at[0, 0]),
                (dot_hbm.at[rows16], table.at[0, 1]),
                (pk_hbm.at[:, lanes(core * wide, wide)], prefix.at[0]),
                (pv_hbm.at[:, lanes(core * wide, wide)], prefix.at[1]),
            )
        )
    ]
    for h in range(HEADS):
        slots[h][:, :, REACH] = jnp.zeros((2, 4, SPAN, WIDTH), F32)
    meet([sibling] + z_peers + x_peers + y_peers)

    pair = [
        start(columns(u, other), kv[u].at[mine * 2 + core], pair_sem.at[u], sibling)
        for u in range(UNITS)
    ]
    for copy in own:
        copy.wait()

    y_copies, gx_copies, f_copies, gf_copies = {}, {}, {}, {}

    def y_pair(col, rr, u, r):
        block = kv[u].at[me.chip(0, col) * 2 + r]
        y_copies[col, rr, u] = [
            start(block, block, y_sem.at[d, col, rr, u], peer) for d, peer in enumerate((up, down))
        ]

    def gather_first(u):
        for rr, r in enumerate((core, other)):
            if rr == 1:
                pair[u].wait_recv()
            block = kv[u].at[mine * 2 + r]
            gx_copies[rr, u] = start(block, block, gx_sem.at[rr, u], across)
            y_pair(0, rr, u, r)

    def forward(col, u):
        for d, (rr, dy, peer) in enumerate(((0, 3, up), (1, 1, down))):
            y_copies[col, rr, u][d].wait_recv()
            block = kv[u].at[me.chip(dy, col) * 2 + (core if rr == 0 else other)]
            f_copies[d, col, u] = start(block, block, f_sem.at[d, col, u], peer)

    def gather_second(u):
        for rr, r in enumerate((core, other)):
            gx_copies[rr, u].wait_recv()
            y_pair(1, rr, u, r)
        forward(0, u)

    def gather_third(u):
        for rr, r in enumerate((core, other)):
            f_copies[rr, 0, u].wait_recv()
            block = kv[u].at[me.chip(2, 0) * 2 + r]
            gf_copies[rr, u] = start(block, block, gf_sem.at[rr, u], across)

    def gather_end(u):
        y_copies[0, 1, u][0].wait_recv()
        y_copies[0, 0, u][1].wait_recv()
        for rr in range(2):
            for d in range(2):
                y_copies[1, rr, u][d].wait_recv()
        for rr in range(2):
            gf_copies[rr, u].wait_recv()

    lane_row = lax.rem(lax.broadcasted_iota(jnp.int32, (1, LANES), 1), SPAN)
    key_row = lax.broadcasted_iota(jnp.int32, (REACH * SPAN, 1), 0)
    prefix_seen = lax.broadcasted_iota(jnp.int32, (PREFIX, 1), 0) < plen_ref[0]
    places = [index_ref[PLACES + s] for s in range(4)]

    def queries(h, s):
        w, r = s // 2, (s % 2) * SPAN

        def heads_of(ref):
            return jnp.concatenate(
                [
                    ref[w, r : r + SPAN, (h * GROUP + g) * WIDTH : (h * GROUP + g + 1) * WIDTH]
                    for g in range(GROUP)
                ],
                axis=0,
            )

        def row_of(which):
            part = table[w, which, h * GROUP : (h + 1) * GROUP, :][:, r : r + SPAN]
            return jnp.concatenate([part[g : g + 1] for g in range(GROUP)], axis=1)

        return heads_of(q_ref), heads_of(g_ref), row_of(0) * LOG2E, row_of(1)

    def tile(keys, values, seen, q, grad, norm, dot):
        st = nt(keys, q)
        p = jnp.where(seen, jnp.exp2(st * (SCALE * LOG2E) - norm), 0.0)
        dv = nn(p.astype(BF16), grad)
        dp = nt(values, grad)
        ds = (p * (dp - dot)).astype(BF16)
        dk = nn(ds, q)
        dq = tn(ds, keys)
        return dk * SCALE, dv, dq

    def prefix_tile(h, s):
        at = slice(h * WIDTH, (h + 1) * WIDTH)
        dk, dv, dq = tile(prefix[0, :, at], prefix[1, :, at], prefix_seen, *queries(h, s))
        if s == 0:
            dp_ref[0, :, at] = dk
            dp_ref[1, :, at] = dv
        else:
            dp_ref[0, :, at] += dk
            dp_ref[1, :, at] += dv
        dq_prefix[h, s] = dq

    def look(u, s):
        for n in range(REACH):
            window[u % 2, n * SPAN : (n + 1) * SPAN] = kv[u][
                index_ref[BLOCKS + s * REACH + n], index_ref[HALVES + s * REACH + n]
            ]
        return window[u % 2]

    def give_slots(h, i, s, value):
        for n in range(REACH):
            slots[h][i, s, n] = value[n * SPAN : (n + 1) * SPAN]

    def value_tile(h, s):
        q, grad, norm, dot = queries(h, s)
        upper = places[s] * SPAN + lane_row
        lower = jnp.zeros_like(upper)
        for d in range(8):
            begin = index_ref[STARTS + d]
            lower = jnp.maximum(lower, jnp.where(begin <= upper, begin, 0))
        pos = (places[s] - BACK) * SPAN + key_row
        seen = (pos >= lower) & (pos <= upper)
        st = nt(look(2 * h, s), q)
        p = jnp.where(seen, jnp.exp2(st * (SCALE * LOG2E) - norm), 0.0)
        probs[s] = p
        give_slots(h, 1, s, nn(p.astype(BF16), grad))

    def key_tile(h, s):
        w, r = s // 2, (s % 2) * SPAN
        q, grad, norm, dot = queries(h, s)
        keys = look(2 * h, s)
        dp = nt(look(2 * h + 1, s), grad)
        ds = (probs[s] * (dp - dot)).astype(BF16)
        give_slots(h, 0, s, nn(ds, q) * SCALE)
        dq = tn(ds, keys) + dq_prefix[h, s]
        dq = (dq * SCALE).astype(BF16)
        for g in range(GROUP):
            dq_stage[w, r : r + SPAN, (h * GROUP + g) * WIDTH : (h * GROUP + g + 1) * WIDTH] = dq[
                g * SPAN : (g + 1) * SPAN
            ]

    backs, keeps = [], []

    def give_dq(h):
        at = slice(h * GROUP * WIDTH, (h + 1) * GROUP * WIDTH)
        to = lanes(core * HALF + h * GROUP * WIDTH, GROUP * WIDTH)
        keeps.append(fetch(dq_stage.at[0, :, at], dq_ref.at[:, to], keep_sem.at[h]))
        backs.append(start(dq_stage.at[1, :, at], dq_ref.at[:, to], back_sem.at[h], sibling))

    def own_part(u, chip, r, n):
        total = None
        for s in range(4):
            at = index_ref[SLOTS + (chip * 4 + r * 2 + n) * 4 + s]
            term = slots[u // 2][u % 2, s, at]
            total = term if total is None else total + term
        return total

    pieces = [(n, slice(n * SPAN, (n + 1) * SPAN)) for n in range(2)]
    ways = tuple(enumerate(((up, 1), (down, 3))))
    cross, edge, near, far, mid, over, last = {}, {}, {}, {}, {}, {}, {}

    def send_cross(u):
        for r in range(2):
            for n, at in pieces:
                xf_out[r, u, at] = own_part(u, me.chip(2, 1), r, n).astype(BF16)
            cross[r, u] = start(xf_out.at[r, u], xf_buf.at[r, u], xf_sem.at[r, u], across)

    def send_edge(u):
        for r in range(2):
            for d, (peer, dy) in ways:
                for n, at in pieces:
                    edge_out[d, r, u, at] = own_part(u, me.chip(dy, 1), r, n).astype(BF16)
                edge[d, r, u] = start(
                    edge_out.at[d, r, u], e_buf.at[d, r, u], e_sem.at[d, r, u], peer
                )

    def send_near(u):
        for d, (peer, dy) in ways:
            for n, at in pieces:
                near_out[d, u, at] = own_part(u, me.chip(dy, 0), d, n).astype(BF16)
            near[d, u] = start(near_out.at[d, u], b_buf.at[d, u], b_sem.at[d, u], peer)

    def send_far(u):
        for d, (peer, dy) in ways:
            r = 1 - d
            cross[r, u].wait_recv()
            for n, at in pieces:
                far_out[d, u, at] = (
                    own_part(u, me.chip(2, 0), r, n) + xf_buf[r, u, at].astype(F32)
                ).astype(BF16)
            far[d, u] = start(far_out.at[d, u], a_buf.at[d, u], a_sem.at[d, u], peer)

    def pass_on(u):
        for d, (peer, dy) in ways:
            far[d, u].wait_recv()
            for n, at in pieces:
                c_out[d, u, at] = (
                    own_part(u, me.chip(dy, 0), 1 - d, n) + a_buf[d, u, at].astype(F32)
                ).astype(BF16)
            mid[d, u] = start(c_out.at[d, u], c_buf.at[d, u], c_sem.at[d, u], peer)

    def over_x(u):
        for r in range(2):
            for d in range(2):
                edge[d, r, u].wait_recv()
            for n, at in pieces:
                x_out[r, u, at] = (
                    own_part(u, me.chip(0, 1), r, n)
                    + e_buf[0, r, u, at].astype(F32)
                    + e_buf[1, r, u, at].astype(F32)
                ).astype(BF16)
            over[r, u] = start(x_out.at[r, u], x_buf.at[r, u], x_sem.at[r, u], across)

    def hold(u):
        for r in range(2):
            d = 1 - r
            mid[d, u].wait_recv()
            near[1 - d, u].wait_recv()
            for n, at in pieces:
                held[r, u, at] = (
                    own_part(u, mine, r, n)
                    + c_buf[d, u, at].astype(F32)
                    + b_buf[1 - d, u, at].astype(F32)
                )

    def finish(u):
        for r in range(2):
            over[r, u].wait_recv()
        last_out[u] = (held[other, u] + x_buf[other, u].astype(F32)).astype(BF16)
        last[u] = start(last_out.at[u], last_buf.at[u], last_sem.at[u], sibling)
        ref = (dk_ref, dv_ref)[u % 2]
        ref[:, lanes((core * 2 + u // 2) * WIDTH, WIDTH)] = (
            held[core, u] + x_buf[core, u].astype(F32)
        ).astype(BF16)

    def take_last(u):
        last[u].wait_recv()
        ref = (dk_ref, dv_ref)[u % 2]
        ref[:, lanes((other * 2 + u // 2) * WIDTH, WIDTH)] = last_buf[u]

    def reduce_first(u):
        send_cross(u)
        send_edge(u)
        send_near(u)

    def reduce_second(u):
        send_far(u)
        over_x(u)

    def reduce_last(u):
        hold(u)
        finish(u)

    def sixteen(i, size):
        return pl.ds(pl.multiple_of(i * size, size), size)

    steps = {}

    def prefix_z():
        steps["z"] = [
            start(dp_ref.at[:, sixteen(lax.rem(me.z + n + 1, 4), 64)], z_buf.at[n], z_sem.at[n], p)
            for n, p in enumerate(z_peers)
        ]

    def prefix_x():
        for copy in steps["z"]:
            copy.wait_recv()
        z_sum[...] = dp_ref[:, sixteen(me.z, 64)] + z_buf[0] + z_buf[1] + z_buf[2]
        steps["x"] = [
            start(z_sum.at[:, sixteen(lax.rem(me.x + n + 1, 4), 16)], px_buf.at[n], px_sem.at[n], p)
            for n, p in enumerate(x_peers)
        ]

    def prefix_y():
        for copy in steps["x"]:
            copy.wait_recv()
        piece = z_sum[:, sixteen(me.x, 16)] + px_buf[0] + px_buf[1] + px_buf[2]
        px_sum[...] = piece
        py_buf[me.y] = piece
        steps["y"] = [
            start(px_sum, py_buf.at[me.y], py_sem.at[n], p) for n, p in enumerate(y_peers)
        ]

    def prefix_ax():
        for copy in steps["y"]:
            copy.wait_recv()
        fin[me.z, me.x] = ((py_buf[0] + py_buf[1]) + py_buf[2]) + py_buf[3]
        block = fin.at[me.z, me.x]
        steps["ax"] = [start(block, block, ax_sem.at[n], p) for n, p in enumerate(x_peers)]

    def prefix_az():
        for copy in steps["ax"]:
            copy.wait_recv()
        block = fin.at[me.z]
        steps["az"] = [start(block, block, az_sem.at[n], p) for n, p in enumerate(z_peers)]

    def prefix_ac():
        for copy in steps["az"]:
            copy.wait_recv()
        steps["ac"] = start(fin, fin_other, ac_sem, sibling)

    def prefix_lay(src, which):
        at = lanes(which * wide, wide)
        for z in range(4):
            for x in range(4):
                rows = slice(z * 64 + x * 16, z * 64 + x * 16 + 16)
                dpk_ref[rows, at] = src[z, x, 0]
                dpv_ref[rows, at] = src[z, x, 1]

    gather_first(0)
    swaps = [
        start(src, dst, swap_sem.at[n], sibling)
        for n, (src, dst) in enumerate(
            (
                (q_hbm.at[:, lanes(other * HALF, HALF)], q_ref.at[1]),
                (g_hbm.at[:, lanes(other * HALF, HALF)], g_ref.at[1]),
                (norm_hbm.at[other16], table.at[1, 0]),
                (dot_hbm.at[other16], table.at[1, 1]),
            )
        )
    ]
    for copy in loads:
        copy.wait()
    gather_first(1)
    prefix_tile(0, 0)
    prefix_tile(0, 1)
    prefix_tile(1, 0)
    gather_second(0)
    prefix_tile(1, 1)
    for copy in swaps:
        copy.wait_recv()
    prefix_tile(0, 2)
    prefix_tile(0, 3)
    gather_second(1)
    gather_first(2)
    prefix_tile(1, 2)
    prefix_tile(1, 3)
    gather_third(0)
    prefix_z()
    gather_end(0)
    value_tile(0, 0)
    gather_third(1)
    value_tile(0, 1)
    gather_second(2)
    gather_first(3)
    value_tile(0, 2)
    prefix_x()
    value_tile(0, 3)
    reduce_first(1)
    gather_end(1)
    gather_third(2)
    key_tile(0, 0)
    gather_second(3)
    prefix_y()
    key_tile(0, 1)
    reduce_second(1)
    key_tile(0, 2)
    gather_third(3)
    prefix_ax()
    key_tile(0, 3)
    reduce_first(0)
    give_dq(0)
    gather_end(2)
    value_tile(1, 0)
    pass_on(1)
    value_tile(1, 1)
    reduce_second(0)
    prefix_az()
    value_tile(1, 2)
    value_tile(1, 3)
    reduce_first(3)
    gather_end(3)
    key_tile(1, 0)
    pass_on(0)
    reduce_last(1)
    prefix_ac()
    key_tile(1, 1)
    reduce_second(3)
    key_tile(1, 2)
    prefix_lay(fin, core)
    key_tile(1, 3)
    reduce_first(2)
    give_dq(1)
    pass_on(3)
    reduce_second(2)
    reduce_last(0)
    steps["ac"].wait_recv()
    prefix_lay(fin_other, other)
    pass_on(2)
    reduce_last(3)
    take_last(1)
    take_last(0)
    take_last(3)
    reduce_last(2)
    take_last(2)
    for copy in backs:
        copy.wait_recv()
    for copy in keeps:
        copy.wait()
    for copy in sent:
        copy.wait_send()


def run(index, plen, q, g, norm, dot, k, v, pk, pv):
    smem = pl.BlockSpec(memory_space=pltpu.SMEM)
    vmem = pl.BlockSpec(memory_space=pltpu.VMEM)
    anywhere = pl.BlockSpec(memory_space=pl.ANY)
    dma = pltpu.SemaphoreType.DMA
    unit = (ROWS, WIDTH)
    wide = HEADS * WIDTH
    return pl.pallas_call(
        fused_kernel,
        out_shape=(
            jax.ShapeDtypeStruct((ROWS, 2 * HALF), BF16),
            jax.ShapeDtypeStruct((ROWS, 2 * wide), BF16),
            jax.ShapeDtypeStruct((ROWS, 2 * wide), BF16),
            jax.ShapeDtypeStruct((PREFIX, 2 * wide), F32),
            jax.ShapeDtypeStruct((PREFIX, 2 * wide), F32),
        ),
        in_specs=[smem] * 2 + [anywhere] * 8,
        out_specs=(anywhere, vmem, vmem, vmem, vmem),
        scratch_shapes=[
            pltpu.VMEM((2, ROWS, HALF), BF16),
            pltpu.VMEM((2, ROWS, HALF), BF16),
            pltpu.VMEM((2, 2, 16, ROWS), F32),
            pltpu.VMEM((2, PREFIX, wide), BF16),
            pltpu.VMEM((16, 2, SPAN, WIDTH), BF16),
            pltpu.VMEM((16, 2, SPAN, WIDTH), BF16),
            pltpu.VMEM((16, 2, SPAN, WIDTH), BF16),
            pltpu.VMEM((16, 2, SPAN, WIDTH), BF16),
            pltpu.VMEM((2, REACH * SPAN, WIDTH), BF16),
            pltpu.VMEM((4, REACH * SPAN, LANES), F32),
            pltpu.VMEM((2, 4, REACH + 1, SPAN, WIDTH), F32),
            pltpu.VMEM((2, 4, REACH + 1, SPAN, WIDTH), F32),
            pltpu.VMEM((HEADS, 4, LANES, WIDTH), F32),
            pltpu.VMEM((2, ROWS, HALF), BF16),
            pltpu.VMEM((2, PREFIX, wide), F32),
            pltpu.VMEM((2, UNITS) + unit, BF16),
            pltpu.VMEM((2, UNITS) + unit, BF16),
            pltpu.VMEM((2, 2, UNITS) + unit, BF16),
            pltpu.VMEM((2, UNITS) + unit, BF16),
            pltpu.VMEM((2, UNITS) + unit, BF16),
            pltpu.VMEM((2, UNITS) + unit, BF16),
            pltpu.VMEM((2, 2, UNITS) + unit, BF16),
            pltpu.VMEM((2, UNITS) + unit, BF16),
            pltpu.VMEM((2, UNITS) + unit, BF16),
            pltpu.VMEM((2, UNITS) + unit, BF16),
            pltpu.VMEM((2, UNITS) + unit, BF16),
            pltpu.VMEM((2, UNITS) + unit, BF16),
            pltpu.VMEM((2, UNITS) + unit, F32),
            pltpu.VMEM((UNITS,) + unit, BF16),
            pltpu.VMEM((UNITS,) + unit, BF16),
            pltpu.VMEM((3, 2, 64, wide), F32),
            pltpu.VMEM((2, 64, wide), F32),
            pltpu.VMEM((3, 2, 16, wide), F32),
            pltpu.VMEM((2, 16, wide), F32),
            pltpu.VMEM((4, 2, 16, wide), F32),
            pltpu.VMEM((4, 4, 2, 16, wide), F32),
            pltpu.VMEM((4, 4, 2, 16, wide), F32),
            dma((6,)),
            dma((UNITS,)),
            dma((UNITS, 2)),
            dma((4, 2)),
            dma((2, 2, 2, UNITS, 2)),
            dma((2, 2, UNITS, 2)),
            dma((2, UNITS, 2)),
            dma((2, UNITS, 2)),
            dma((HEADS,)),
            dma((HEADS, 2)),
            dma((2, UNITS, 2)),
            dma((2, UNITS, 2)),
            dma((2, 2, UNITS, 2)),
            dma((2, UNITS, 2)),
            dma((2, UNITS, 2)),
            dma((2, UNITS, 2)),
            dma((UNITS, 2)),
            dma((3, 2)),
            dma((3, 2)),
            dma((3, 2)),
            dma((3, 2)),
            dma((3, 2)),
            dma((2,)),
        ],
        compiler_params=pltpu.CompilerParams(
            collective_id=0, has_side_effects=True, vmem_limit_bytes=60 * 1024 * 1024
        ),
        name="pack_grads",
    )(index, plen, q, g, norm, dot, k, v, pk, pv)


def copy_kernel(*refs):
    count = (len(refs) - 2) // 3
    ins, outs, held = refs[:count], refs[count : 2 * count], refs[2 * count : 3 * count]
    in_sem, out_sem = refs[-2:]
    parts = []
    for n in range(count):
        pieces = 4 if n == 0 else 1
        size = ins[n].shape[0] // pieces
        for part in range(pieces):
            parts.append((n, pl.ds(part * size, size)))
    first = [
        pltpu.make_async_copy(ins[n].at[rows], held[n].at[rows], in_sem.at[i])
        for i, (n, rows) in enumerate(parts)
    ]
    second = [
        pltpu.make_async_copy(held[n].at[rows], outs[n].at[rows], out_sem.at[i])
        for i, (n, rows) in enumerate(parts)
    ]
    for copy in first:
        copy.start()
    for copy, onward in zip(first, second):
        copy.wait()
        onward.start()
    for copy in second:
        copy.wait()


def settle(arrays):
    anywhere = pl.BlockSpec(memory_space=pl.ANY)
    return pl.pallas_call(
        copy_kernel,
        out_shape=tuple(jax.ShapeDtypeStruct(a.shape, a.dtype) for a in arrays),
        in_specs=[anywhere] * len(arrays),
        out_specs=(anywhere,) * len(arrays),
        scratch_shapes=[pltpu.VMEM(a.shape, a.dtype) for a in arrays]
        + [pltpu.SemaphoreType.DMA((len(arrays) + 3,)), pltpu.SemaphoreType.DMA((len(arrays) + 3,))],
        name="results",
    )(*arrays)


def local(
    query_matrix,
    key_matrix,
    value_matrix,
    output_gradient,
    log_softmax_norm,
    output_dot_rows,
    shared_prefix_keys,
    shared_prefix_values,
    prefix_len,
    segments,
    span_order,
):
    results = run(
        prepare(span_order[0], segments),
        prefix_len,
        query_matrix[0],
        output_gradient[0],
        log_softmax_norm[0],
        output_dot_rows[0],
        key_matrix.reshape(2, SPAN, KEY_VALUE_HEADS * WIDTH),
        value_matrix.reshape(2, SPAN, KEY_VALUE_HEADS * WIDTH),
        shared_prefix_keys,
        shared_prefix_values,
    )
    dq, dk, dv, dpk, dpv = settle(results)
    return dq[None], dk[None], dv[None], dpk, dpv


def solution(mesh):
    return jax.shard_map(
        local,
        mesh=mesh,
        in_specs=(
            P("dp", "blk", None),
            P("dp", "blk", None),
            P("dp", "blk", None),
            P("dp", "blk", None),
            P("dp", None, "blk"),
            P("dp", None, "blk"),
            P(),
            P(),
            P("dp"),
            P("dp", None),
            P("dp", None),
        ),
        out_specs=(P("dp", "blk", None), P("dp", "blk", None), P("dp", "blk", None), P(), P()),
        check_vma=False,
    )
```

```python
import functools

import jax
import jax.numpy as jnp
from jax import lax
from jax.experimental import pallas as pl
from jax.experimental.pallas import tpu as pltpu
from jax.sharding import PartitionSpec as P

QUERY_HEADS = 32
KEY_VALUE_HEADS = 4
GROUP = QUERY_HEADS // KEY_VALUE_HEADS
WIDTH = 128
SPAN = 96
ROWS = 192
PREFIX = 256
TOKENS = 3072
SPANS = 32
BACK = 8
REACH = BACK + 1
STARTS, PLACES, BLOCKS, HALVES, SLOTS = 0, 8, 16, 64, 128
HEADS = 2
UNITS = 2 * HEADS
DIRECT_GATHER, DIRECT_REDUCE = (0, 1, 2, 3), (0, 1, 2, 3)
HALF = HEADS * GROUP * WIDTH
SCALE = WIDTH**-0.5
LOG2E = 1.4426950408889634
LANES = GROUP * SPAN
MESH = pl.DeviceIdType.MESH
BF16 = jnp.bfloat16
F32 = jnp.float32


def nt(a, b):
    return lax.dot_general(a, b, (((1,), (1,)), ((), ())), preferred_element_type=F32)


def nn(a, b):
    return lax.dot_general(a, b, (((1,), (0,)), ((), ())), preferred_element_type=F32)


def tn(a, b):
    return lax.dot_general(a, b, (((0,), (0,)), ((), ())), preferred_element_type=F32)


class Place:
    def __init__(self):
        self.dp, self.blk = lax.axis_index("dp"), lax.axis_index("blk")
        self.x_lo, self.z = self.dp // 4, lax.rem(self.dp, 4)
        self.y, self.x_hi = self.blk // 4, lax.rem(self.blk // 2, 2)
        self.core = lax.rem(self.blk, 2)
        self.x = self.x_hi * 2 + self.x_lo

    def at(self, dx=0, dy=0, dz=0, other=False):
        x = lax.rem(self.x + dx, 4)
        y = lax.rem(self.y + dy, 4)
        z = lax.rem(self.z + dz, 4)
        core = 1 - self.core if other else self.core
        return (lax.rem(x, 2) * 4 + z, (y * 2 + x // 2) * 2 + core)

    def chip(self, dy, col):
        x_hi = self.x_hi if col == 0 else 1 - self.x_hi
        return lax.rem(self.y + dy, 4) * 2 + x_hi


def meet(peers):
    barrier = pltpu.get_barrier_semaphore()
    for peer in peers:
        pl.semaphore_signal(barrier, inc=1, device_id=peer, device_id_type=MESH)
    pl.semaphore_wait(barrier, len(peers))


def remote(src, dst, send, recv, peer):
    return pltpu.make_async_remote_copy(
        src_ref=src, dst_ref=dst, send_sem=send, recv_sem=recv, device_id=peer, device_id_type=MESH
    )


def lanes(start, size):
    return pl.ds(pl.multiple_of(start, WIDTH), size)


def prepare_kernel(order_ref, segments_ref, out_ref, inverse):
    mine = lax.axis_index("blk") // 2
    core = lax.rem(lax.axis_index("blk"), 2)
    segments = segments_ref[...]
    out_ref[STARTS] = 0
    for d in range(1, 8):
        out_ref[STARTS + d] = jnp.sum((segments < d).astype(jnp.int32))
    for t in range(SPANS):
        inverse[order_ref[t]] = t
    places = []
    for s in range(4):
        place = order_ref[mine * 4 + (core if s < 2 else 1 - core) * 2 + s % 2]
        places.append(place)
        out_ref[PLACES + s] = place
        for n in range(REACH):
            t = inverse[jnp.maximum(place - BACK + n, 0)]
            out_ref[BLOCKS + s * REACH + n] = lax.shift_right_logical(t, 1)
            out_ref[HALVES + s * REACH + n] = t & 1
    for t in range(SPANS):
        there = order_ref[t]
        for s in range(4):
            at = there - places[s] + BACK
            out_ref[SLOTS + t * 4 + s] = jnp.where((at >= 0) & (at <= BACK), at, REACH)


def prepare(order, segments):
    smem = pl.BlockSpec(memory_space=pltpu.SMEM)
    return pl.pallas_call(
        prepare_kernel,
        out_shape=jax.ShapeDtypeStruct((256,), jnp.int32),
        in_specs=[smem, pl.BlockSpec(memory_space=pltpu.VMEM)],
        out_specs=smem,
        scratch_shapes=[pltpu.SMEM((SPANS,), jnp.int32)],
        name="tables",
    )(order, segments)


def fused_kernel(
    index_ref,
    plen_ref,
    q_hbm,
    g_hbm,
    norm_hbm,
    dot_hbm,
    k_hbm,
    v_hbm,
    pk_hbm,
    pv_hbm,
    dq_ref,
    dk_ref,
    dv_ref,
    dpk_ref,
    dpv_ref,
    q_ref,
    g_ref,
    table,
    prefix,
    kv_0,
    kv_1,
    kv_2,
    kv_3,
    window,
    probs,
    slots_0,
    slots_1,
    dq_prefix,
    dq_stage,
    dp_ref,
    far_out,
    near_out,
    edge_out,
    xf_out,
    a_buf,
    b_buf,
    e_buf,
    c_buf,
    c_out,
    x_buf,
    x_out,
    xf_buf,
    held,
    last_out,
    last_buf,
    z_buf,
    z_sum,
    px_buf,
    px_sum,
    py_buf,
    fin,
    fin_other,
    load_sem,
    own_sem,
    pair_sem,
    swap_sem,
    y_sem,
    f_sem,
    gx_sem,
    gf_sem,
    keep_sem,
    back_sem,
    a_sem,
    b_sem,
    e_sem,
    c_sem,
    x_sem,
    xf_sem,
    last_sem,
    z_sem,
    px_sem,
    py_sem,
    ax_sem,
    az_sem,
    ac_sem,
):
    me = Place()
    core, other = me.core, 1 - me.core
    mine = me.chip(0, 0)
    sibling = me.at(other=True)
    up, down, opposite, across = me.at(dy=1), me.at(dy=3), me.at(dy=2), me.at(dx=2)
    z_peers = [me.at(dz=d) for d in (1, 2, 3)]
    x_peers = [me.at(dx=d) for d in (1, 2, 3)]
    y_peers = [me.at(dy=d) for d in (1, 2, 3)]
    half = lanes(core * HALF, HALF)
    wide = HEADS * WIDTH
    sources, kv, slots = (k_hbm, v_hbm), (kv_0, kv_1, kv_2, kv_3), (slots_0, slots_1)
    sent = []

    def start(src, dst, sem, peer):
        copy = remote(src, dst, sem.at[0], sem.at[1], peer)
        copy.start()
        sent.append(copy)
        return copy

    def fetch(src, dst, sem):
        copy = pltpu.make_async_copy(src, dst, sem)
        copy.start()
        return copy

    def columns(u, which):
        return sources[u % 2].at[:, :, lanes((which * 2 + u // 2) * WIDTH, WIDTH)]

    own = [
        fetch(columns(u, core), kv[u].at[mine * 2 + core], own_sem.at[u]) for u in range(UNITS)
    ]
    rows16 = pl.ds(pl.multiple_of(core * 16, 16), 16)
    other16 = pl.ds(pl.multiple_of(other * 16, 16), 16)
    loads = [
        fetch(src, dst, load_sem.at[n])
        for n, (src, dst) in enumerate(
            (
                (q_hbm.at[:, half], q_ref.at[0]),
                (g_hbm.at[:, half], g_ref.at[0]),
                (norm_hbm.at[rows16], table.at[0, 0]),
                (dot_hbm.at[rows16], table.at[0, 1]),
                (pk_hbm.at[:, lanes(core * wide, wide)], prefix.at[0]),
                (pv_hbm.at[:, lanes(core * wide, wide)], prefix.at[1]),
            )
        )
    ]
    for h in range(HEADS):
        slots[h][:, :, REACH] = jnp.zeros((2, 4, SPAN, WIDTH), F32)
    meet([sibling] + z_peers + x_peers + y_peers)

    pair = [
        start(columns(u, other), kv[u].at[mine * 2 + core], pair_sem.at[u], sibling)
        for u in range(UNITS)
    ]
    for copy in own:
        copy.wait()

    y_copies, gx_copies, f_copies, gf_copies = {}, {}, {}, {}

    def y_pair(col, rr, u, r):
        block = kv[u].at[me.chip(0, col) * 2 + r]
        y_copies[col, rr, u] = [
            start(block, block, y_sem.at[d, col, rr, u], peer) for d, peer in enumerate((up, down))
        ]

    def gather_first(u):
        for rr, r in enumerate((core, other)):
            if rr == 1:
                pair[u].wait_recv()
            block = kv[u].at[mine * 2 + r]
            gx_copies[rr, u] = start(block, block, gx_sem.at[rr, u], across)
            y_pair(0, rr, u, r)
            if u in DIRECT_GATHER:
                f_copies[rr, 0, u] = start(block, block, f_sem.at[rr, 0, u], opposite)

    def forward(col, u):
        for d, (rr, dy, peer) in enumerate(((0, 3, up), (1, 1, down))):
            y_copies[col, rr, u][d].wait_recv()
            block = kv[u].at[me.chip(dy, col) * 2 + (core if rr == 0 else other)]
            f_copies[d, col, u] = start(block, block, f_sem.at[d, col, u], peer)

    def gather_second(u):
        for rr, r in enumerate((core, other)):
            gx_copies[rr, u].wait_recv()
            y_pair(1, rr, u, r)
        if u not in DIRECT_GATHER:
            forward(0, u)

    def gather_third(u):
        for rr, r in enumerate((core, other)):
            f_copies[rr, 0, u].wait_recv()
            block = kv[u].at[me.chip(2, 0) * 2 + r]
            gf_copies[rr, u] = start(block, block, gf_sem.at[rr, u], across)

    def gather_end(u):
        y_copies[0, 1, u][0].wait_recv()
        y_copies[0, 0, u][1].wait_recv()
        if u in DIRECT_GATHER:
            y_copies[0, 0, u][0].wait_recv()
            y_copies[0, 1, u][1].wait_recv()
        for rr in range(2):
            for d in range(2):
                y_copies[1, rr, u][d].wait_recv()
        for rr in range(2):
            gf_copies[rr, u].wait_recv()

    lane_row = lax.rem(lax.broadcasted_iota(jnp.int32, (1, LANES), 1), SPAN)
    key_row = lax.broadcasted_iota(jnp.int32, (REACH * SPAN, 1), 0)
    prefix_seen = lax.broadcasted_iota(jnp.int32, (PREFIX, 1), 0) < plen_ref[0]
    places = [index_ref[PLACES + s] for s in range(4)]

    def queries(h, s):
        w, r = s // 2, (s % 2) * SPAN

        def heads_of(ref):
            return jnp.concatenate(
                [
                    ref[w, r : r + SPAN, (h * GROUP + g) * WIDTH : (h * GROUP + g + 1) * WIDTH]
                    for g in range(GROUP)
                ],
                axis=0,
            )

        def row_of(which):
            part = table[w, which, h * GROUP : (h + 1) * GROUP, :][:, r : r + SPAN]
            return jnp.concatenate([part[g : g + 1] for g in range(GROUP)], axis=1)

        return heads_of(q_ref), heads_of(g_ref), row_of(0) * LOG2E, row_of(1)

    def tile(keys, values, seen, q, grad, norm, dot):
        st = nt(keys, q)
        p = jnp.where(seen, jnp.exp2(st * (SCALE * LOG2E) - norm), 0.0)
        dv = nn(p.astype(BF16), grad)
        dp = nt(values, grad)
        ds = (p * (dp - dot)).astype(BF16)
        dk = nn(ds, q)
        dq = tn(ds, keys)
        return dk * SCALE, dv, dq

    def prefix_tile(h, s):
        at = slice(h * WIDTH, (h + 1) * WIDTH)
        dk, dv, dq = tile(prefix[0, :, at], prefix[1, :, at], prefix_seen, *queries(h, s))
        if s == 0:
            dp_ref[0, :, at] = dk
            dp_ref[1, :, at] = dv
        else:
            dp_ref[0, :, at] += dk
            dp_ref[1, :, at] += dv
        dq_prefix[h, s] = dq

    def look(u, s):
        for n in range(REACH):
            window[u % 2, n * SPAN : (n + 1) * SPAN] = kv[u][
                index_ref[BLOCKS + s * REACH + n], index_ref[HALVES + s * REACH + n]
            ]
        return window[u % 2]

    def give_slots(h, i, s, value):
        for n in range(REACH):
            slots[h][i, s, n] = value[n * SPAN : (n + 1) * SPAN]

    def value_tile(h, s):
        q, grad, norm, dot = queries(h, s)
        upper = places[s] * SPAN + lane_row
        lower = jnp.zeros_like(upper)
        for d in range(8):
            begin = index_ref[STARTS + d]
            lower = jnp.maximum(lower, jnp.where(begin <= upper, begin, 0))
        pos = (places[s] - BACK) * SPAN + key_row
        seen = (pos >= lower) & (pos <= upper)
        st = nt(look(2 * h, s), q)
        p = jnp.where(seen, jnp.exp2(st * (SCALE * LOG2E) - norm), 0.0)
        probs[s] = p
        give_slots(h, 1, s, nn(p.astype(BF16), grad))

    def key_tile(h, s):
        w, r = s // 2, (s % 2) * SPAN
        q, grad, norm, dot = queries(h, s)
        keys = look(2 * h, s)
        dp = nt(look(2 * h + 1, s), grad)
        ds = (probs[s] * (dp - dot)).astype(BF16)
        give_slots(h, 0, s, nn(ds, q) * SCALE)
        dq = tn(ds, keys) + dq_prefix[h, s]
        dq = (dq * SCALE).astype(BF16)
        for g in range(GROUP):
            dq_stage[w, r : r + SPAN, (h * GROUP + g) * WIDTH : (h * GROUP + g + 1) * WIDTH] = dq[
                g * SPAN : (g + 1) * SPAN
            ]

    backs, keeps = [], []

    def give_dq(h):
        at = slice(h * GROUP * WIDTH, (h + 1) * GROUP * WIDTH)
        to = lanes(core * HALF + h * GROUP * WIDTH, GROUP * WIDTH)
        keeps.append(fetch(dq_stage.at[0, :, at], dq_ref.at[:, to], keep_sem.at[h]))
        backs.append(start(dq_stage.at[1, :, at], dq_ref.at[:, to], back_sem.at[h], sibling))

    def own_part(u, chip, r, n):
        total = None
        for s in range(4):
            at = index_ref[SLOTS + (chip * 4 + r * 2 + n) * 4 + s]
            term = slots[u // 2][u % 2, s, at]
            total = term if total is None else total + term
        return total

    pieces = [(n, slice(n * SPAN, (n + 1) * SPAN)) for n in range(2)]
    ways = tuple(enumerate(((up, 1), (down, 3))))
    cross, edge, near, far, mid, over, last = {}, {}, {}, {}, {}, {}, {}

    def send_cross(u):
        for r in range(2):
            for n, at in pieces:
                xf_out[r, u, at] = own_part(u, me.chip(2, 1), r, n).astype(BF16)
            cross[r, u] = start(xf_out.at[r, u], xf_buf.at[r, u], xf_sem.at[r, u], across)

    def send_edge(u):
        for r in range(2):
            for d, (peer, dy) in ways:
                for n, at in pieces:
                    edge_out[d, r, u, at] = own_part(u, me.chip(dy, 1), r, n).astype(BF16)
                edge[d, r, u] = start(
                    edge_out.at[d, r, u], e_buf.at[d, r, u], e_sem.at[d, r, u], peer
                )

    def send_near(u):
        for d, (peer, dy) in ways:
            for n, at in pieces:
                near_out[d, u, at] = own_part(u, me.chip(dy, 0), d, n).astype(BF16)
            near[d, u] = start(near_out.at[d, u], b_buf.at[d, u], b_sem.at[d, u], peer)

    def send_far(u):
        for d, (peer, dy) in ways:
            r = 1 - d
            cross[r, u].wait_recv()
            for n, at in pieces:
                far_out[d, u, at] = (
                    own_part(u, me.chip(2, 0), r, n) + xf_buf[r, u, at].astype(F32)
                ).astype(BF16)
            to = opposite if u in DIRECT_REDUCE else peer
            far[d, u] = start(far_out.at[d, u], a_buf.at[d, u], a_sem.at[d, u], to)

    def send_mid(u):
        for d, (peer, dy) in ways:
            if u not in DIRECT_REDUCE:
                far[d, u].wait_recv()
            for n, at in pieces:
                value = own_part(u, me.chip(dy, 0), 1 - d, n)
                if u not in DIRECT_REDUCE:
                    value = value + a_buf[d, u, at].astype(F32)
                c_out[d, u, at] = value.astype(BF16)
            mid[d, u] = start(c_out.at[d, u], c_buf.at[d, u], c_sem.at[d, u], peer)

    def pass_on(u):
        if u not in DIRECT_REDUCE:
            send_mid(u)

    def over_x(u):
        for r in range(2):
            for d in range(2):
                edge[d, r, u].wait_recv()
            for n, at in pieces:
                x_out[r, u, at] = (
                    own_part(u, me.chip(0, 1), r, n)
                    + e_buf[0, r, u, at].astype(F32)
                    + e_buf[1, r, u, at].astype(F32)
                ).astype(BF16)
            over[r, u] = start(x_out.at[r, u], x_buf.at[r, u], x_sem.at[r, u], across)

    def hold(u):
        for r in range(2):
            d = 1 - r
            mid[d, u].wait_recv()
            near[1 - d, u].wait_recv()
            if u in DIRECT_REDUCE:
                far[d, u].wait_recv()
            for n, at in pieces:
                value = (
                    own_part(u, mine, r, n)
                    + c_buf[d, u, at].astype(F32)
                    + b_buf[1 - d, u, at].astype(F32)
                )
                if u in DIRECT_REDUCE:
                    value = value + a_buf[d, u, at].astype(F32)
                held[r, u, at] = value

    def finish(u):
        for r in range(2):
            over[r, u].wait_recv()
        last_out[u] = (held[other, u] + x_buf[other, u].astype(F32)).astype(BF16)
        last[u] = start(last_out.at[u], last_buf.at[u], last_sem.at[u], sibling)
        ref = (dk_ref, dv_ref)[u % 2]
        ref[:, lanes((core * 2 + u // 2) * WIDTH, WIDTH)] = (
            held[core, u] + x_buf[core, u].astype(F32)
        ).astype(BF16)

    def take_last(u):
        last[u].wait_recv()
        ref = (dk_ref, dv_ref)[u % 2]
        ref[:, lanes((other * 2 + u // 2) * WIDTH, WIDTH)] = last_buf[u]

    def reduce_first(u):
        send_cross(u)
        send_edge(u)
        send_near(u)
        if u in DIRECT_REDUCE:
            send_mid(u)

    def reduce_second(u):
        send_far(u)
        over_x(u)

    def reduce_last(u):
        hold(u)
        finish(u)

    def sixteen(i, size):
        return pl.ds(pl.multiple_of(i * size, size), size)

    steps = {}

    def prefix_z():
        steps["z"] = [
            start(dp_ref.at[:, sixteen(lax.rem(me.z + n + 1, 4), 64)], z_buf.at[n], z_sem.at[n], p)
            for n, p in enumerate(z_peers)
        ]

    def prefix_x():
        for copy in steps["z"]:
            copy.wait_recv()
        z_sum[...] = dp_ref[:, sixteen(me.z, 64)] + z_buf[0] + z_buf[1] + z_buf[2]
        steps["x"] = [
            start(z_sum.at[:, sixteen(lax.rem(me.x + n + 1, 4), 16)], px_buf.at[n], px_sem.at[n], p)
            for n, p in enumerate(x_peers)
        ]

    def prefix_y():
        for copy in steps["x"]:
            copy.wait_recv()
        piece = z_sum[:, sixteen(me.x, 16)] + px_buf[0] + px_buf[1] + px_buf[2]
        px_sum[...] = piece
        py_buf[me.y] = piece
        steps["y"] = [
            start(px_sum, py_buf.at[me.y], py_sem.at[n], p) for n, p in enumerate(y_peers)
        ]

    def prefix_ax():
        for copy in steps["y"]:
            copy.wait_recv()
        fin[me.z, me.x] = ((py_buf[0] + py_buf[1]) + py_buf[2]) + py_buf[3]
        block = fin.at[me.z, me.x]
        steps["ax"] = [start(block, block, ax_sem.at[n], p) for n, p in enumerate(x_peers)]

    def prefix_az():
        for copy in steps["ax"]:
            copy.wait_recv()
        block = fin.at[me.z]
        steps["az"] = [start(block, block, az_sem.at[n], p) for n, p in enumerate(z_peers)]

    def prefix_ac():
        for copy in steps["az"]:
            copy.wait_recv()
        steps["ac"] = start(fin, fin_other, ac_sem, sibling)

    def prefix_lay(src, which):
        at = lanes(which * wide, wide)
        for z in range(4):
            for x in range(4):
                rows = slice(z * 64 + x * 16, z * 64 + x * 16 + 16)
                dpk_ref[rows, at] = src[z, x, 0]
                dpv_ref[rows, at] = src[z, x, 1]

    gather_first(0)
    swaps = [
        start(src, dst, swap_sem.at[n], sibling)
        for n, (src, dst) in enumerate(
            (
                (q_hbm.at[:, lanes(other * HALF, HALF)], q_ref.at[1]),
                (g_hbm.at[:, lanes(other * HALF, HALF)], g_ref.at[1]),
                (norm_hbm.at[other16], table.at[1, 0]),
                (dot_hbm.at[other16], table.at[1, 1]),
            )
        )
    ]
    for copy in loads:
        copy.wait()
    gather_first(1)
    prefix_tile(0, 0)
    prefix_tile(0, 1)
    prefix_tile(1, 0)
    gather_second(0)
    gather_first(2)
    prefix_tile(1, 1)
    for copy in swaps:
        copy.wait_recv()
    prefix_tile(0, 2)
    gather_third(0)
    gather_second(1)
    gather_first(3)
    prefix_tile(0, 3)
    prefix_tile(1, 2)
    prefix_tile(1, 3)
    prefix_z()
    gather_end(0)
    value_tile(0, 0)
    gather_third(1)
    value_tile(0, 1)
    gather_second(2)
    value_tile(0, 2)
    value_tile(0, 3)
    reduce_first(1)
    gather_second(3)
    gather_third(2)
    gather_end(1)
    key_tile(0, 0)
    prefix_x()
    key_tile(0, 1)
    gather_third(3)
    key_tile(0, 2)
    reduce_second(1)
    key_tile(0, 3)
    reduce_first(0)
    give_dq(0)
    prefix_y()
    gather_end(2)
    value_tile(1, 0)
    value_tile(1, 1)
    pass_on(1)
    value_tile(1, 2)
    reduce_second(0)
    value_tile(1, 3)
    reduce_first(3)
    prefix_ax()
    gather_end(3)
    key_tile(1, 0)
    pass_on(0)
    key_tile(1, 1)
    reduce_last(1)
    key_tile(1, 2)
    prefix_az()
    key_tile(1, 3)
    reduce_first(2)
    give_dq(1)
    reduce_second(3)
    prefix_ac()
    reduce_second(2)
    reduce_last(0)
    pass_on(3)
    take_last(1)
    take_last(0)
    prefix_lay(fin, core)
    pass_on(2)
    reduce_last(3)
    steps["ac"].wait_recv()
    prefix_lay(fin_other, other)
    reduce_last(2)
    take_last(3)
    take_last(2)
    for copy in backs:
        copy.wait_recv()
    for copy in keeps:
        copy.wait()
    for copy in sent:
        copy.wait_send()


def run(index, plen, q, g, norm, dot, k, v, pk, pv):
    smem = pl.BlockSpec(memory_space=pltpu.SMEM)
    vmem = pl.BlockSpec(memory_space=pltpu.VMEM)
    anywhere = pl.BlockSpec(memory_space=pl.ANY)
    dma = pltpu.SemaphoreType.DMA
    unit = (ROWS, WIDTH)
    wide = HEADS * WIDTH
    return pl.pallas_call(
        fused_kernel,
        out_shape=(
            jax.ShapeDtypeStruct((ROWS, 2 * HALF), BF16),
            jax.ShapeDtypeStruct((ROWS, 2 * wide), BF16),
            jax.ShapeDtypeStruct((ROWS, 2 * wide), BF16),
            jax.ShapeDtypeStruct((PREFIX, 2 * wide), F32),
            jax.ShapeDtypeStruct((PREFIX, 2 * wide), F32),
        ),
        in_specs=[smem] * 2 + [anywhere] * 8,
        out_specs=(anywhere, vmem, vmem, vmem, vmem),
        scratch_shapes=[
            pltpu.VMEM((2, ROWS, HALF), BF16),
            pltpu.VMEM((2, ROWS, HALF), BF16),
            pltpu.VMEM((2, 2, 16, ROWS), F32),
            pltpu.VMEM((2, PREFIX, wide), BF16),
            pltpu.VMEM((16, 2, SPAN, WIDTH), BF16),
            pltpu.VMEM((16, 2, SPAN, WIDTH), BF16),
            pltpu.VMEM((16, 2, SPAN, WIDTH), BF16),
            pltpu.VMEM((16, 2, SPAN, WIDTH), BF16),
            pltpu.VMEM((2, REACH * SPAN, WIDTH), BF16),
            pltpu.VMEM((4, REACH * SPAN, LANES), F32),
            pltpu.VMEM((2, 4, REACH + 1, SPAN, WIDTH), F32),
            pltpu.VMEM((2, 4, REACH + 1, SPAN, WIDTH), F32),
            pltpu.VMEM((HEADS, 4, LANES, WIDTH), F32),
            pltpu.VMEM((2, ROWS, HALF), BF16),
            pltpu.VMEM((2, PREFIX, wide), F32),
            pltpu.VMEM((2, UNITS) + unit, BF16),
            pltpu.VMEM((2, UNITS) + unit, BF16),
            pltpu.VMEM((2, 2, UNITS) + unit, BF16),
            pltpu.VMEM((2, UNITS) + unit, BF16),
            pltpu.VMEM((2, UNITS) + unit, BF16),
            pltpu.VMEM((2, UNITS) + unit, BF16),
            pltpu.VMEM((2, 2, UNITS) + unit, BF16),
            pltpu.VMEM((2, UNITS) + unit, BF16),
            pltpu.VMEM((2, UNITS) + unit, BF16),
            pltpu.VMEM((2, UNITS) + unit, BF16),
            pltpu.VMEM((2, UNITS) + unit, BF16),
            pltpu.VMEM((2, UNITS) + unit, BF16),
            pltpu.VMEM((2, UNITS) + unit, F32),
            pltpu.VMEM((UNITS,) + unit, BF16),
            pltpu.VMEM((UNITS,) + unit, BF16),
            pltpu.VMEM((3, 2, 64, wide), F32),
            pltpu.VMEM((2, 64, wide), F32),
            pltpu.VMEM((3, 2, 16, wide), F32),
            pltpu.VMEM((2, 16, wide), F32),
            pltpu.VMEM((4, 2, 16, wide), F32),
            pltpu.VMEM((4, 4, 2, 16, wide), F32),
            pltpu.VMEM((4, 4, 2, 16, wide), F32),
            dma((6,)),
            dma((UNITS,)),
            dma((UNITS, 2)),
            dma((4, 2)),
            dma((2, 2, 2, UNITS, 2)),
            dma((2, 1, UNITS, 2)),
            dma((2, UNITS, 2)),
            dma((2, UNITS, 2)),
            dma((HEADS,)),
            dma((HEADS, 2)),
            dma((2, UNITS, 2)),
            dma((2, UNITS, 2)),
            dma((2, 2, UNITS, 2)),
            dma((2, UNITS, 2)),
            dma((2, UNITS, 2)),
            dma((2, UNITS, 2)),
            dma((UNITS, 2)),
            dma((3, 2)),
            dma((3, 2)),
            dma((3, 2)),
            dma((3, 2)),
            dma((3, 2)),
            dma((2,)),
        ],
        compiler_params=pltpu.CompilerParams(
            collective_id=0, has_side_effects=True, vmem_limit_bytes=60 * 1024 * 1024
        ),
        name="pack_grads",
    )(index, plen, q, g, norm, dot, k, v, pk, pv)


def copy_kernel(*refs):
    count = (len(refs) - 2) // 3
    ins, outs, held = refs[:count], refs[count : 2 * count], refs[2 * count : 3 * count]
    in_sem, out_sem = refs[-2:]
    parts = []
    for n in range(count):
        pieces = 4 if n == 0 else 1
        size = ins[n].shape[0] // pieces
        for part in range(pieces):
            parts.append((n, pl.ds(part * size, size)))
    first = [
        pltpu.make_async_copy(ins[n].at[rows], held[n].at[rows], in_sem.at[i])
        for i, (n, rows) in enumerate(parts)
    ]
    second = [
        pltpu.make_async_copy(held[n].at[rows], outs[n].at[rows], out_sem.at[i])
        for i, (n, rows) in enumerate(parts)
    ]
    for copy in first:
        copy.start()
    for copy, onward in zip(first, second):
        copy.wait()
        onward.start()
    for copy in second:
        copy.wait()


def settle(arrays):
    anywhere = pl.BlockSpec(memory_space=pl.ANY)
    return pl.pallas_call(
        copy_kernel,
        out_shape=tuple(jax.ShapeDtypeStruct(a.shape, a.dtype) for a in arrays),
        in_specs=[anywhere] * len(arrays),
        out_specs=(anywhere,) * len(arrays),
        scratch_shapes=[pltpu.VMEM(a.shape, a.dtype) for a in arrays]
        + [pltpu.SemaphoreType.DMA((len(arrays) + 3,)), pltpu.SemaphoreType.DMA((len(arrays) + 3,))],
        name="results",
    )(*arrays)


def local(
    query_matrix,
    key_matrix,
    value_matrix,
    output_gradient,
    log_softmax_norm,
    output_dot_rows,
    shared_prefix_keys,
    shared_prefix_values,
    prefix_len,
    segments,
    span_order,
):
    results = run(
        prepare(span_order[0], segments),
        prefix_len,
        query_matrix[0],
        output_gradient[0],
        log_softmax_norm[0],
        output_dot_rows[0],
        key_matrix.reshape(2, SPAN, KEY_VALUE_HEADS * WIDTH),
        value_matrix.reshape(2, SPAN, KEY_VALUE_HEADS * WIDTH),
        shared_prefix_keys,
        shared_prefix_values,
    )
    dq, dk, dv, dpk, dpv = settle(results)
    return dq[None], dk[None], dv[None], dpk, dpv


def solution(mesh):
    return jax.shard_map(
        local,
        mesh=mesh,
        in_specs=(
            P("dp", "blk", None),
            P("dp", "blk", None),
            P("dp", "blk", None),
            P("dp", "blk", None),
            P("dp", None, "blk"),
            P("dp", None, "blk"),
            P(),
            P(),
            P("dp"),
            P("dp", None),
            P("dp", None),
        ),
        out_specs=(P("dp", "blk", None), P("dp", "blk", None), P("dp", "blk", None), P(), P()),
        check_vma=False,
    )
```

```python
import functools

import jax
import jax.numpy as jnp
from jax import lax
from jax.experimental import pallas as pl
from jax.experimental.pallas import tpu as pltpu
from jax.sharding import PartitionSpec as P

QUERY_HEADS = 32
KEY_VALUE_HEADS = 4
GROUP = QUERY_HEADS // KEY_VALUE_HEADS
WIDTH = 128
SPAN = 96
ROWS = 192
PREFIX = 256
TOKENS = 3072
SPANS = 32
BACK = 8
REACH = BACK + 1
STARTS, PLACES, BLOCKS, HALVES, SLOTS = 0, 8, 16, 64, 128
HEADS = 2
UNITS = 2 * HEADS
SPLIT = (0,)
HALF = HEADS * GROUP * WIDTH
SCALE = WIDTH**-0.5
LOG2E = 1.4426950408889634
LANES = GROUP * SPAN
MESH = pl.DeviceIdType.MESH
BF16 = jnp.bfloat16
F32 = jnp.float32


def nt(a, b):
    return lax.dot_general(a, b, (((1,), (1,)), ((), ())), preferred_element_type=F32)


def nn(a, b):
    return lax.dot_general(a, b, (((1,), (0,)), ((), ())), preferred_element_type=F32)


def tn(a, b):
    return lax.dot_general(a, b, (((0,), (0,)), ((), ())), preferred_element_type=F32)


class Place:
    def __init__(self):
        self.dp, self.blk = lax.axis_index("dp"), lax.axis_index("blk")
        self.x_lo, self.z = self.dp // 4, lax.rem(self.dp, 4)
        self.y, self.x_hi = self.blk // 4, lax.rem(self.blk // 2, 2)
        self.core = lax.rem(self.blk, 2)
        self.x = self.x_hi * 2 + self.x_lo

    def at(self, dx=0, dy=0, dz=0, other=False):
        x = lax.rem(self.x + dx, 4)
        y = lax.rem(self.y + dy, 4)
        z = lax.rem(self.z + dz, 4)
        core = 1 - self.core if other else self.core
        return (lax.rem(x, 2) * 4 + z, (y * 2 + x // 2) * 2 + core)

    def chip(self, dy, col):
        x_hi = self.x_hi if col == 0 else 1 - self.x_hi
        return lax.rem(self.y + dy, 4) * 2 + x_hi


def meet(peers):
    barrier = pltpu.get_barrier_semaphore()
    for peer in peers:
        pl.semaphore_signal(barrier, inc=1, device_id=peer, device_id_type=MESH)
    pl.semaphore_wait(barrier, len(peers))


def remote(src, dst, send, recv, peer):
    return pltpu.make_async_remote_copy(
        src_ref=src, dst_ref=dst, send_sem=send, recv_sem=recv, device_id=peer, device_id_type=MESH
    )


def lanes(start, size):
    return pl.ds(pl.multiple_of(start, WIDTH), size)


def prepare_kernel(order_ref, segments_ref, out_ref, inverse):
    mine = lax.axis_index("blk") // 2
    core = lax.rem(lax.axis_index("blk"), 2)
    segments = segments_ref[...]
    out_ref[STARTS] = 0
    for d in range(1, 8):
        out_ref[STARTS + d] = jnp.sum((segments < d).astype(jnp.int32))
    for t in range(SPANS):
        inverse[order_ref[t]] = t
    places = []
    for s in range(4):
        place = order_ref[mine * 4 + (core if s < 2 else 1 - core) * 2 + s % 2]
        places.append(place)
        out_ref[PLACES + s] = place
        for n in range(REACH):
            t = inverse[jnp.maximum(place - BACK + n, 0)]
            out_ref[BLOCKS + s * REACH + n] = lax.shift_right_logical(t, 1)
            out_ref[HALVES + s * REACH + n] = t & 1
    for t in range(SPANS):
        there = order_ref[t]
        for s in range(4):
            at = there - places[s] + BACK
            out_ref[SLOTS + t * 4 + s] = jnp.where((at >= 0) & (at <= BACK), at, REACH)


def prepare(order, segments):
    smem = pl.BlockSpec(memory_space=pltpu.SMEM)
    return pl.pallas_call(
        prepare_kernel,
        out_shape=jax.ShapeDtypeStruct((256,), jnp.int32),
        in_specs=[smem, pl.BlockSpec(memory_space=pltpu.VMEM)],
        out_specs=smem,
        scratch_shapes=[pltpu.SMEM((SPANS,), jnp.int32)],
        name="tables",
    )(order, segments)


def fused_kernel(
    index_ref,
    plen_ref,
    q_hbm,
    g_hbm,
    norm_hbm,
    dot_hbm,
    k_hbm,
    v_hbm,
    pk_hbm,
    pv_hbm,
    dq_ref,
    dk_ref,
    dv_ref,
    dpk_ref,
    dpv_ref,
    q_ref,
    g_ref,
    table,
    prefix,
    kv_0,
    kv_1,
    kv_2,
    kv_3,
    window,
    probs,
    slots_0,
    slots_1,
    dq_prefix,
    dq_stage,
    dp_ref,
    far_out,
    near_out,
    edge_out,
    xf_out,
    a_buf,
    b_buf,
    e_buf,
    x_buf,
    x_out,
    xf_buf,
    last_out,
    last_buf,
    z_buf,
    z_sum,
    px_buf,
    px_sum,
    py_buf,
    fin,
    fin_other,
    load_sem,
    own_sem,
    pair_sem,
    swap_sem,
    y_sem,
    f_sem,
    gx_sem,
    gf_sem,
    keep_sem,
    back_sem,
    a_sem,
    b_sem,
    e_sem,
    x_sem,
    xf_sem,
    last_sem,
    z_sem,
    px_sem,
    py_sem,
    ax_sem,
    az_sem,
    ac_sem,
):
    me = Place()
    core, other = me.core, 1 - me.core
    mine = me.chip(0, 0)
    sibling = me.at(other=True)
    up, down, opposite, across = me.at(dy=1), me.at(dy=3), me.at(dy=2), me.at(dx=2)
    z_peers = [me.at(dz=d) for d in (1, 2, 3)]
    x_peers = [me.at(dx=d) for d in (1, 2, 3)]
    y_peers = [me.at(dy=d) for d in (1, 2, 3)]
    half = lanes(core * HALF, HALF)
    wide = HEADS * WIDTH
    sources, kv, slots = (k_hbm, v_hbm), (kv_0, kv_1, kv_2, kv_3), (slots_0, slots_1)
    sent = []

    def start(src, dst, sem, peer):
        copy = remote(src, dst, sem.at[0], sem.at[1], peer)
        copy.start()
        sent.append(copy)
        return copy

    def fetch(src, dst, sem):
        copy = pltpu.make_async_copy(src, dst, sem)
        copy.start()
        return copy

    def columns(u, which):
        return sources[u % 2].at[:, :, lanes((which * 2 + u // 2) * WIDTH, WIDTH)]

    own = [
        fetch(columns(u, core), kv[u].at[mine * 2 + core], own_sem.at[u]) for u in range(UNITS)
    ]
    rows16 = pl.ds(pl.multiple_of(core * 16, 16), 16)
    other16 = pl.ds(pl.multiple_of(other * 16, 16), 16)
    loads = [
        fetch(src, dst, load_sem.at[n])
        for n, (src, dst) in enumerate(
            (
                (q_hbm.at[:, half], q_ref.at[0]),
                (g_hbm.at[:, half], g_ref.at[0]),
                (norm_hbm.at[rows16], table.at[0, 0]),
                (dot_hbm.at[rows16], table.at[0, 1]),
                (pk_hbm.at[:, lanes(core * wide, wide)], prefix.at[0]),
                (pv_hbm.at[:, lanes(core * wide, wide)], prefix.at[1]),
            )
        )
    ]
    for h in range(HEADS):
        slots[h][:, :, REACH] = jnp.zeros((2, 4, SPAN, WIDTH), F32)
    meet([sibling] + z_peers + x_peers + y_peers)

    pair = [
        start(columns(u, other), kv[u].at[mine * 2 + core], pair_sem.at[u], sibling)
        for u in range(UNITS)
    ]
    for copy in own:
        copy.wait()

    y_copies, gx_copies, f_copies, gf_copies = {}, {}, {}, {}

    def parts(u):
        return ((0, core), (1, other)) if u in SPLIT else ((0, None),)

    def view(u, chip, r):
        at = pl.ds(chip * 2, 2) if r is None else pl.ds(chip * 2 + r, 1)
        return kv[u].at[at]

    def y_pair(col, rr, u, block):
        y_copies[col, rr, u] = [
            start(block, block, y_sem.at[d, col, rr, u], peer) for d, peer in enumerate((up, down))
        ]

    def gather_first(u):
        for rr, r in parts(u):
            if rr == 1 or r is None:
                pair[u].wait_recv()
            block = view(u, mine, r)
            gx_copies[rr, u] = start(block, block, gx_sem.at[rr, u], across)
            f_copies[rr, u] = start(block, block, f_sem.at[rr, u], opposite)
            y_pair(0, rr, u, block)

    def gather_second(u):
        for rr, r in parts(u):
            gx_copies[rr, u].wait_recv()
            y_pair(1, rr, u, view(u, me.chip(0, 1), r))

    def gather_third(u):
        for rr, r in parts(u):
            f_copies[rr, u].wait_recv()
            block = view(u, me.chip(2, 0), r)
            gf_copies[rr, u] = start(block, block, gf_sem.at[rr, u], across)

    def gather_end(u):
        for rr, r in parts(u):
            for col in range(2):
                for d in range(2):
                    y_copies[col, rr, u][d].wait_recv()
            gf_copies[rr, u].wait_recv()

    lane_row = lax.rem(lax.broadcasted_iota(jnp.int32, (1, LANES), 1), SPAN)
    key_row = lax.broadcasted_iota(jnp.int32, (REACH * SPAN, 1), 0)
    prefix_seen = lax.broadcasted_iota(jnp.int32, (PREFIX, 1), 0) < plen_ref[0]
    places = [index_ref[PLACES + s] for s in range(4)]

    def queries(h, s):
        w, r = s // 2, (s % 2) * SPAN

        def heads_of(ref):
            return jnp.concatenate(
                [
                    ref[w, r : r + SPAN, (h * GROUP + g) * WIDTH : (h * GROUP + g + 1) * WIDTH]
                    for g in range(GROUP)
                ],
                axis=0,
            )

        def row_of(which):
            part = table[w, which, h * GROUP : (h + 1) * GROUP, :][:, r : r + SPAN]
            return jnp.concatenate([part[g : g + 1] for g in range(GROUP)], axis=1)

        return heads_of(q_ref), heads_of(g_ref), row_of(0) * LOG2E, row_of(1)

    def tile(keys, values, seen, q, grad, norm, dot):
        st = nt(keys, q)
        p = jnp.where(seen, jnp.exp2(st * (SCALE * LOG2E) - norm), 0.0)
        dv = nn(p.astype(BF16), grad)
        dp = nt(values, grad)
        ds = (p * (dp - dot)).astype(BF16)
        dk = nn(ds, q)
        dq = tn(ds, keys)
        return dk * SCALE, dv, dq

    def prefix_tile(h, s):
        at = slice(h * WIDTH, (h + 1) * WIDTH)
        dk, dv, dq = tile(prefix[0, :, at], prefix[1, :, at], prefix_seen, *queries(h, s))
        if s == 0:
            dp_ref[0, :, at] = dk
            dp_ref[1, :, at] = dv
        else:
            dp_ref[0, :, at] += dk
            dp_ref[1, :, at] += dv
        dq_prefix[h, s] = dq

    def look(u, s):
        for n in range(REACH):
            window[u % 2, n * SPAN : (n + 1) * SPAN] = kv[u][
                index_ref[BLOCKS + s * REACH + n], index_ref[HALVES + s * REACH + n]
            ]
        return window[u % 2]

    def give_slots(h, i, s, value):
        for n in range(REACH):
            slots[h][i, s, n] = value[n * SPAN : (n + 1) * SPAN]

    def value_tile(h, s):
        q, grad, norm, dot = queries(h, s)
        upper = places[s] * SPAN + lane_row
        lower = jnp.zeros_like(upper)
        for d in range(8):
            begin = index_ref[STARTS + d]
            lower = jnp.maximum(lower, jnp.where(begin <= upper, begin, 0))
        pos = (places[s] - BACK) * SPAN + key_row
        seen = (pos >= lower) & (pos <= upper)
        st = nt(look(2 * h, s), q)
        p = jnp.where(seen, jnp.exp2(st * (SCALE * LOG2E) - norm), 0.0)
        probs[s] = p
        give_slots(h, 1, s, nn(p.astype(BF16), grad))

    def key_tile(h, s):
        w, r = s // 2, (s % 2) * SPAN
        q, grad, norm, dot = queries(h, s)
        keys = look(2 * h, s)
        dp = nt(look(2 * h + 1, s), grad)
        ds = (probs[s] * (dp - dot)).astype(BF16)
        give_slots(h, 0, s, nn(ds, q) * SCALE)
        dq = tn(ds, keys) + dq_prefix[h, s]
        dq = (dq * SCALE).astype(BF16)
        for g in range(GROUP):
            dq_stage[w, r : r + SPAN, (h * GROUP + g) * WIDTH : (h * GROUP + g + 1) * WIDTH] = dq[
                g * SPAN : (g + 1) * SPAN
            ]

    backs, keeps = [], []

    def give_dq(h):
        at = slice(h * GROUP * WIDTH, (h + 1) * GROUP * WIDTH)
        to = lanes(core * HALF + h * GROUP * WIDTH, GROUP * WIDTH)
        keeps.append(fetch(dq_stage.at[0, :, at], dq_ref.at[:, to], keep_sem.at[h]))
        backs.append(start(dq_stage.at[1, :, at], dq_ref.at[:, to], back_sem.at[h], sibling))

    def own_part(u, chip, r, n):
        total = None
        for s in range(4):
            at = index_ref[SLOTS + (chip * 4 + r * 2 + n) * 4 + s]
            term = slots[u // 2][u % 2, s, at]
            total = term if total is None else total + term
        return total

    pieces = [(r, n, slice(n * SPAN, (n + 1) * SPAN)) for r in range(2) for n in range(2)]
    ways = tuple(enumerate(((up, 1), (down, 3))))
    cross, edge, near, far, over, last = {}, {}, {}, {}, {}, {}

    def send_cross(u):
        for r, n, at in pieces:
            xf_out[u, r, at] = own_part(u, me.chip(2, 1), r, n).astype(BF16)
        cross[u] = start(xf_out.at[u], xf_buf.at[u], xf_sem.at[u], across)

    def send_edge(u):
        for d, (peer, dy) in ways:
            for r, n, at in pieces:
                edge_out[d, u, r, at] = own_part(u, me.chip(dy, 1), r, n).astype(BF16)
            edge[d, u] = start(edge_out.at[d, u], e_buf.at[d, u], e_sem.at[d, u], peer)

    def send_near(u):
        for d, (peer, dy) in ways:
            for r, n, at in pieces:
                near_out[d, u, r, at] = own_part(u, me.chip(dy, 0), r, n).astype(BF16)
            near[d, u] = start(near_out.at[d, u], b_buf.at[d, u], b_sem.at[d, u], peer)

    def send_far(u):
        cross[u].wait_recv()
        for r, n, at in pieces:
            far_out[u, r, at] = (
                own_part(u, me.chip(2, 0), r, n) + xf_buf[u, r, at].astype(F32)
            ).astype(BF16)
        far[u] = start(far_out.at[u], a_buf.at[u], a_sem.at[u], opposite)

    def over_x(u):
        for d in range(2):
            edge[d, u].wait_recv()
        for r, n, at in pieces:
            x_out[u, r, at] = (
                own_part(u, me.chip(0, 1), r, n)
                + e_buf[0, u, r, at].astype(F32)
                + e_buf[1, u, r, at].astype(F32)
            ).astype(BF16)
        over[u] = start(x_out.at[u], x_buf.at[u], x_sem.at[u], across)

    def whole_sum(u, r, n, at):
        return (
            own_part(u, mine, r, n)
            + b_buf[0, u, r, at].astype(F32)
            + b_buf[1, u, r, at].astype(F32)
            + a_buf[u, r, at].astype(F32)
            + x_buf[u, r, at].astype(F32)
        ).astype(BF16)

    def reduce_last(u):
        for copy in (near[0, u], near[1, u], far[u], over[u]):
            copy.wait_recv()
        for r, n, at in pieces[:2]:
            last_out[u, at] = whole_sum(u, other, n, at)
        last[u] = start(last_out.at[u], last_buf.at[u], last_sem.at[u], sibling)
        ref = (dk_ref, dv_ref)[u % 2]
        for r, n, at in pieces[:2]:
            ref[at, lanes((core * 2 + u // 2) * WIDTH, WIDTH)] = whole_sum(u, core, n, at)

    def take_last(u):
        last[u].wait_recv()
        ref = (dk_ref, dv_ref)[u % 2]
        ref[:, lanes((other * 2 + u // 2) * WIDTH, WIDTH)] = last_buf[u]

    def reduce_first(u):
        send_cross(u)
        send_edge(u)
        send_near(u)

    def reduce_second(u):
        send_far(u)
        over_x(u)

    def sixteen(i, size):
        return pl.ds(pl.multiple_of(i * size, size), size)

    steps = {}

    def prefix_z():
        steps["z"] = [
            start(dp_ref.at[:, sixteen(lax.rem(me.z + n + 1, 4), 64)], z_buf.at[n], z_sem.at[n], p)
            for n, p in enumerate(z_peers)
        ]

    def prefix_x():
        for copy in steps["z"]:
            copy.wait_recv()
        z_sum[...] = dp_ref[:, sixteen(me.z, 64)] + z_buf[0] + z_buf[1] + z_buf[2]
        steps["x"] = [
            start(z_sum.at[:, sixteen(lax.rem(me.x + n + 1, 4), 16)], px_buf.at[n], px_sem.at[n], p)
            for n, p in enumerate(x_peers)
        ]

    def prefix_y():
        for copy in steps["x"]:
            copy.wait_recv()
        piece = z_sum[:, sixteen(me.x, 16)] + px_buf[0] + px_buf[1] + px_buf[2]
        px_sum[...] = piece
        py_buf[me.y] = piece
        steps["y"] = [
            start(px_sum, py_buf.at[me.y], py_sem.at[n], p) for n, p in enumerate(y_peers)
        ]

    def prefix_ax():
        for copy in steps["y"]:
            copy.wait_recv()
        fin[me.z, me.x] = ((py_buf[0] + py_buf[1]) + py_buf[2]) + py_buf[3]
        block = fin.at[me.z, me.x]
        steps["ax"] = [start(block, block, ax_sem.at[n], p) for n, p in enumerate(x_peers)]

    def prefix_az():
        for copy in steps["ax"]:
            copy.wait_recv()
        block = fin.at[me.z]
        steps["az"] = [start(block, block, az_sem.at[n], p) for n, p in enumerate(z_peers)]

    def prefix_ac():
        for copy in steps["az"]:
            copy.wait_recv()
        steps["ac"] = start(fin, fin_other, ac_sem, sibling)

    def prefix_lay(src, which):
        at = lanes(which * wide, wide)
        for z in range(4):
            for x in range(4):
                rows = slice(z * 64 + x * 16, z * 64 + x * 16 + 16)
                dpk_ref[rows, at] = src[z, x, 0]
                dpv_ref[rows, at] = src[z, x, 1]

    gather_first(0)
    swaps = [
        start(src, dst, swap_sem.at[n], sibling)
        for n, (src, dst) in enumerate(
            (
                (q_hbm.at[:, lanes(other * HALF, HALF)], q_ref.at[1]),
                (g_hbm.at[:, lanes(other * HALF, HALF)], g_ref.at[1]),
                (norm_hbm.at[other16], table.at[1, 0]),
                (dot_hbm.at[other16], table.at[1, 1]),
            )
        )
    ]
    for copy in loads:
        copy.wait()
    gather_first(1)
    prefix_tile(0, 0)
    prefix_tile(0, 1)
    prefix_tile(1, 0)
    gather_second(0)
    gather_first(2)
    prefix_tile(1, 1)
    for copy in swaps:
        copy.wait_recv()
    prefix_tile(0, 2)
    gather_third(0)
    gather_second(1)
    gather_first(3)
    prefix_tile(0, 3)
    prefix_tile(1, 2)
    prefix_tile(1, 3)
    prefix_z()
    gather_end(0)
    value_tile(0, 0)
    gather_third(1)
    value_tile(0, 1)
    value_tile(0, 2)
    gather_second(2)
    value_tile(0, 3)
    reduce_first(1)
    gather_second(3)
    gather_end(1)
    key_tile(0, 0)
    gather_third(2)
    prefix_x()
    key_tile(0, 1)
    key_tile(0, 2)
    gather_third(3)
    reduce_second(1)
    key_tile(0, 3)
    reduce_first(0)
    give_dq(0)
    prefix_y()
    gather_end(2)
    value_tile(1, 0)
    value_tile(1, 1)
    reduce_second(0)
    value_tile(1, 2)
    value_tile(1, 3)
    reduce_first(3)
    prefix_ax()
    gather_end(3)
    key_tile(1, 0)
    reduce_last(1)
    key_tile(1, 1)
    key_tile(1, 2)
    reduce_second(3)
    prefix_az()
    key_tile(1, 3)
    reduce_first(2)
    give_dq(1)
    prefix_ac()
    reduce_second(2)
    reduce_last(0)
    take_last(1)
    take_last(0)
    prefix_lay(fin, core)
    reduce_last(3)
    steps["ac"].wait_recv()
    prefix_lay(fin_other, other)
    reduce_last(2)
    take_last(3)
    take_last(2)
    for copy in backs:
        copy.wait_recv()
    for copy in keeps:
        copy.wait()
    for copy in sent:
        copy.wait_send()


def run(index, plen, q, g, norm, dot, k, v, pk, pv):
    smem = pl.BlockSpec(memory_space=pltpu.SMEM)
    vmem = pl.BlockSpec(memory_space=pltpu.VMEM)
    anywhere = pl.BlockSpec(memory_space=pl.ANY)
    dma = pltpu.SemaphoreType.DMA
    unit = (ROWS, WIDTH)
    wide = HEADS * WIDTH
    return pl.pallas_call(
        fused_kernel,
        out_shape=(
            jax.ShapeDtypeStruct((ROWS, 2 * HALF), BF16),
            jax.ShapeDtypeStruct((ROWS, 2 * wide), BF16),
            jax.ShapeDtypeStruct((ROWS, 2 * wide), BF16),
            jax.ShapeDtypeStruct((PREFIX, 2 * wide), F32),
            jax.ShapeDtypeStruct((PREFIX, 2 * wide), F32),
        ),
        in_specs=[smem] * 2 + [anywhere] * 8,
        out_specs=(anywhere, vmem, vmem, vmem, vmem),
        scratch_shapes=[
            pltpu.VMEM((2, ROWS, HALF), BF16),
            pltpu.VMEM((2, ROWS, HALF), BF16),
            pltpu.VMEM((2, 2, 16, ROWS), F32),
            pltpu.VMEM((2, PREFIX, wide), BF16),
            pltpu.VMEM((16, 2, SPAN, WIDTH), BF16),
            pltpu.VMEM((16, 2, SPAN, WIDTH), BF16),
            pltpu.VMEM((16, 2, SPAN, WIDTH), BF16),
            pltpu.VMEM((16, 2, SPAN, WIDTH), BF16),
            pltpu.VMEM((2, REACH * SPAN, WIDTH), BF16),
            pltpu.VMEM((4, REACH * SPAN, LANES), F32),
            pltpu.VMEM((2, 4, REACH + 1, SPAN, WIDTH), F32),
            pltpu.VMEM((2, 4, REACH + 1, SPAN, WIDTH), F32),
            pltpu.VMEM((HEADS, 4, LANES, WIDTH), F32),
            pltpu.VMEM((2, ROWS, HALF), BF16),
            pltpu.VMEM((2, PREFIX, wide), F32),
            pltpu.VMEM((UNITS, 2) + unit, BF16),
            pltpu.VMEM((2, UNITS, 2) + unit, BF16),
            pltpu.VMEM((2, UNITS, 2) + unit, BF16),
            pltpu.VMEM((UNITS, 2) + unit, BF16),
            pltpu.VMEM((UNITS, 2) + unit, BF16),
            pltpu.VMEM((2, UNITS, 2) + unit, BF16),
            pltpu.VMEM((2, UNITS, 2) + unit, BF16),
            pltpu.VMEM((UNITS, 2) + unit, BF16),
            pltpu.VMEM((UNITS, 2) + unit, BF16),
            pltpu.VMEM((UNITS, 2) + unit, BF16),
            pltpu.VMEM((UNITS,) + unit, BF16),
            pltpu.VMEM((UNITS,) + unit, BF16),
            pltpu.VMEM((3, 2, 64, wide), F32),
            pltpu.VMEM((2, 64, wide), F32),
            pltpu.VMEM((3, 2, 16, wide), F32),
            pltpu.VMEM((2, 16, wide), F32),
            pltpu.VMEM((4, 2, 16, wide), F32),
            pltpu.VMEM((4, 4, 2, 16, wide), F32),
            pltpu.VMEM((4, 4, 2, 16, wide), F32),
            dma((6,)),
            dma((UNITS,)),
            dma((UNITS, 2)),
            dma((4, 2)),
            dma((2, 2, 2, UNITS, 2)),
            dma((2, UNITS, 2)),
            dma((2, UNITS, 2)),
            dma((2, UNITS, 2)),
            dma((HEADS,)),
            dma((HEADS, 2)),
            dma((UNITS, 2)),
            dma((2, UNITS, 2)),
            dma((2, UNITS, 2)),
            dma((UNITS, 2)),
            dma((UNITS, 2)),
            dma((UNITS, 2)),
            dma((3, 2)),
            dma((3, 2)),
            dma((3, 2)),
            dma((3, 2)),
            dma((3, 2)),
            dma((2,)),
        ],
        compiler_params=pltpu.CompilerParams(
            collective_id=0, has_side_effects=True, vmem_limit_bytes=60 * 1024 * 1024
        ),
        name="pack_grads",
    )(index, plen, q, g, norm, dot, k, v, pk, pv)


def copy_kernel(*refs):
    count = (len(refs) - 2) // 3
    ins, outs, held = refs[:count], refs[count : 2 * count], refs[2 * count : 3 * count]
    in_sem, out_sem = refs[-2:]
    parts = []
    for n in range(count):
        pieces = 4 if n == 0 else 1
        size = ins[n].shape[0] // pieces
        for part in range(pieces):
            parts.append((n, pl.ds(part * size, size)))
    first = [
        pltpu.make_async_copy(ins[n].at[rows], held[n].at[rows], in_sem.at[i])
        for i, (n, rows) in enumerate(parts)
    ]
    second = [
        pltpu.make_async_copy(held[n].at[rows], outs[n].at[rows], out_sem.at[i])
        for i, (n, rows) in enumerate(parts)
    ]
    for copy in first:
        copy.start()
    for copy, onward in zip(first, second):
        copy.wait()
        onward.start()
    for copy in second:
        copy.wait()


def settle(arrays):
    anywhere = pl.BlockSpec(memory_space=pl.ANY)
    return pl.pallas_call(
        copy_kernel,
        out_shape=tuple(jax.ShapeDtypeStruct(a.shape, a.dtype) for a in arrays),
        in_specs=[anywhere] * len(arrays),
        out_specs=(anywhere,) * len(arrays),
        scratch_shapes=[pltpu.VMEM(a.shape, a.dtype) for a in arrays]
        + [pltpu.SemaphoreType.DMA((len(arrays) + 3,)), pltpu.SemaphoreType.DMA((len(arrays) + 3,))],
        name="results",
    )(*arrays)


def local(
    query_matrix,
    key_matrix,
    value_matrix,
    output_gradient,
    log_softmax_norm,
    output_dot_rows,
    shared_prefix_keys,
    shared_prefix_values,
    prefix_len,
    segments,
    span_order,
):
    results = run(
        prepare(span_order[0], segments),
        prefix_len,
        query_matrix[0],
        output_gradient[0],
        log_softmax_norm[0],
        output_dot_rows[0],
        key_matrix.reshape(2, SPAN, KEY_VALUE_HEADS * WIDTH),
        value_matrix.reshape(2, SPAN, KEY_VALUE_HEADS * WIDTH),
        shared_prefix_keys,
        shared_prefix_values,
    )
    dq, dk, dv, dpk, dpv = settle(results)
    return dq[None], dk[None], dv[None], dpk, dpv


def solution(mesh):
    return jax.shard_map(
        local,
        mesh=mesh,
        in_specs=(
            P("dp", "blk", None),
            P("dp", "blk", None),
            P("dp", "blk", None),
            P("dp", "blk", None),
            P("dp", None, "blk"),
            P("dp", None, "blk"),
            P(),
            P(),
            P("dp"),
            P("dp", None),
            P("dp", None),
        ),
        out_specs=(P("dp", "blk", None), P("dp", "blk", None), P("dp", "blk", None), P(), P()),
        check_vma=False,
    )
```
